32 devices in a mesh: dp: 4 (over z), row: 4 (over x, core), col: 2 (over y).
Axes of the slice: x: 2, y: 2, z: 4, core: 2. Of those that a mesh axis runs over, the one named last changes fastest.
Arguments:
- latents_in: bfloat16 [8192, 1152], P(('dp', 'row'), 'col'), may hold values from -6 to 6
- text_emb: bfloat16 [960, 1152], P('dp', 'col'), may hold values from -6 to 6
- time_emb: bfloat16 [8, 6, 1152], P('dp', None, 'col'), may hold values from -3 to 3
- shift_table: bfloat16 [6, 1152], P(None, 'col'), may hold values from -3 to 3
- q_weight: bfloat16 [1152, 1152], P('col', 'row'), may hold values from -0.1875 to 0.1875
- k_weight: bfloat16 [1152, 1152], P('col', 'row'), may hold values from -0.1875 to 0.1875
- v_weight: bfloat16 [1152, 1152], P('col', 'row'), may hold values from -0.1875 to 0.1875
- q_bias: bfloat16 [1152], P(('row', 'col')), may hold values from -3 to 3
- v_bias: bfloat16 [1152], P(('row', 'col')), may hold values from -3 to 3
- o_weight: bfloat16 [1152, 1152], P('row', 'col'), may hold values from -0.5 to 0.5
- o_bias: bfloat16 [1152], P('col'), may hold values from -2 to 2
- cq_weight: bfloat16 [1152, 1152], P('col', 'row'), may hold values from -0.1875 to 0.1875
- cq_bias: bfloat16 [1152], P(('row', 'col')), may hold values from -3 to 3
- ck_weight: bfloat16 [1152, 1152], P('col', 'row'), may hold values from -0.1875 to 0.1875
- cv_weight: bfloat16 [1152, 1152], P('col', 'row'), may hold values from -0.1875 to 0.1875
- cv_bias: bfloat16 [1152], P(('row', 'col')), may hold values from -3 to 3
- co_weight: bfloat16 [1152, 1152], P('row', 'col'), may hold values from -0.5 to 0.5
- co_bias: bfloat16 [1152], P('col'), may hold values from -2 to 2
- up_weight: bfloat16 [1152, 4608], P('col', 'row'), may hold values from -0.1875 to 0.1875
- up_bias: bfloat16 [4608], P(('row', 'col')), may hold values from -3 to 3
- down_weight: bfloat16 [4608, 1152], P('row', 'col'), may hold values from -0.09375 to 0.09375
- down_bias: bfloat16 [1152], P('col'), may hold values from -4 to 4
- cotangent: bfloat16 [8192, 1152], P(('dp', 'row'), 'col'), may hold values from -6 to 6
Outputs:
- layer_out: bfloat16 [8192, 1152], P(('dp', 'row'), 'col')
- token_input_gradient: float32 [8192, 1152], P(('dp', 'row'), 'col')
- text_grad: float32 [960, 1152], P('dp', 'col')
- time_grad: float32 [8, 6, 1152], P('dp', None, 'col')
- table_grad: float32 [6, 1152], P(None, 'col')
- q_weight_grad: float32 [1152, 1152], P('col', 'row')
- k_weight_grad: float32 [1152, 1152], P('col', 'row')
- v_weight_grad: float32 [1152, 1152], P('col', 'row')
- q_bias_grad: float32 [1152], P(('row', 'col'))
- v_bias_grad: float32 [1152], P(('row', 'col'))
- o_weight_grad: float32 [1152, 1152], P('row', 'col')
- o_bias_grad: float32 [1152], P('col')
- cq_weight_grad: float32 [1152, 1152], P('col', 'row')
- cq_bias_grad: float32 [1152], P(('row', 'col'))
- ck_weight_grad: float32 [1152, 1152], P('col', 'row')
- cv_weight_grad: float32 [1152, 1152], P('col', 'row')
- cv_bias_grad: float32 [1152], P(('row', 'col'))
- co_weight_grad: float32 [1152, 1152], P('row', 'col')
- co_bias_grad: float32 [1152], P('col')
- up_weight_grad: float32 [1152, 4608], P('col', 'row')
- up_bias_grad: float32 [4608], P(('row', 'col'))
- down_weight_grad: float32 [4608, 1152], P('row', 'col')
- down_bias_grad: float32 [1152], P('col')
The draws below stay inside these ranges and needn't reach their ends.
All inputs are finite; a program needn't handle non-finite values.
Results may differ from the reference program's by a relative error of at most 0.025.
Values may be sent and summed in bfloat16 or wider, within the bound.
No kernel may reach another device: no remote copies, remote signals or barrier semaphores. Data moves between devices by JAX's collectives and lax.ppermute only.
A program may use at most 192 MiB of HBM per device.

```python
import jax
import jax.numpy as jnp
from jax import lax

D = 1152
HEADS = 16
HD = 72
FF = 4608
SEQ = 1024
TXT = 120
LATENTS = 8
TOKENS = 8192
TEXT_ROWS = 960


def block_levels(stream_key, shape, pieces, low, top_value):
    gain, own = 1.0, jax.random.fold_in(stream_key, 6)
    for position, parts in pieces:
        heights = jnp.exp(jax.random.uniform(jax.random.fold_in(own, position), (parts,), jnp.float32, low / len(pieces), top_value / len(pieces)))
        gain = gain * jnp.repeat(heights, shape[position] // parts).reshape([-1 if axis == position else 1 for axis in range(len(shape))])
    return gain


def scatter_about(rng, dims, spread, bound, cuts=(), held_as=jnp.bfloat16):
    factor_of = block_levels(rng, dims, cuts, -0.22, 0.18) if cuts else 1.0
    entries = jax.random.normal(rng, dims, jnp.float32) * spread * factor_of
    return jnp.minimum(jnp.maximum(entries, -bound), bound).astype(held_as)


def setup_inputs(seed: int = 0) -> dict:
    arg_keys = jax.random.split(jax.random.key(seed), 24)
    return {
        "latents_in": scatter_about(arg_keys[0], (TOKENS, D), 1.0, 6.0, ((0, 16), (1, 2))),
        "text_emb": scatter_about(arg_keys[1], (TEXT_ROWS, D), 1.0, 6.0, ((0, 4), (1, 2))),
        "time_emb": scatter_about(arg_keys[2], (LATENTS, 6, D), 0.5, 3.0, ((0, 4), (2, 2))),
        "shift_table": scatter_about(arg_keys[3], (6, D), 0.5, 3.0, ((1, 2),)),
        "q_weight": scatter_about(arg_keys[4], (D, D), D ** -0.5, 0.1875, ((0, 2), (1, 4))),
        "k_weight": scatter_about(arg_keys[5], (D, D), D ** -0.5, 0.1875, ((0, 2), (1, 4))),
        "v_weight": scatter_about(arg_keys[6], (D, D), D ** -0.5, 0.1875, ((0, 2), (1, 4))),
        "q_bias": scatter_about(arg_keys[7], (D,), 0.5, 3.0, ((0, 8),)),
        "v_bias": scatter_about(arg_keys[8], (D,), 0.5, 3.0, ((0, 8),)),
        "o_weight": scatter_about(arg_keys[9], (D, D), (max(D // 8, 4)) ** -0.5, 0.5, ((0, 4), (1, 2))),
        "o_bias": scatter_about(arg_keys[10], (D,), 0.3, 2.0, ((0, 2),)),
        "cq_weight": scatter_about(arg_keys[11], (D, D), D ** -0.5, 0.1875, ((0, 2), (1, 4))),
        "cq_bias": scatter_about(arg_keys[12], (D,), 0.5, 3.0, ((0, 8),)),
        "ck_weight": scatter_about(arg_keys[13], (D, D), D ** -0.5, 0.1875, ((0, 2), (1, 4))),
        "cv_weight": scatter_about(arg_keys[14], (D, D), D ** -0.5, 0.1875, ((0, 2), (1, 4))),
        "cv_bias": scatter_about(arg_keys[15], (D,), 0.5, 3.0, ((0, 8),)),
        "co_weight": scatter_about(arg_keys[16], (D, D), (max(D // 8, 4)) ** -0.5, 0.5, ((0, 4), (1, 2))),
        "co_bias": scatter_about(arg_keys[17], (D,), 0.3, 2.0, ((0, 2),)),
        "up_weight": scatter_about(arg_keys[18], (D, FF), D ** -0.5, 0.1875, ((0, 2), (1, 4))),
        "up_bias": scatter_about(arg_keys[19], (FF,), 0.5, 3.0, ((0, 8),)),
        "down_weight": scatter_about(arg_keys[20], (FF, D), FF ** -0.5, 0.09375, ((0, 4), (1, 2))),
        "down_bias": scatter_about(arg_keys[21], (D,), 1.0, 4.0, ((0, 2),)),
        "cotangent": scatter_about(arg_keys[22], (TOKENS, D), 1.0, 6.0, ((0, 16), (1, 2))),
    }


HIGHEST = lax.Precision.HIGHEST

@jax.custom_vjp
def low(v):
    return lax.optimization_barrier(v.astype(jnp.bfloat16)).astype(jnp.float32)

@jax.custom_vjp
def low_back(v):
    return v

def low_keep(v):
    return (low(v), None)

def low_pass(kept, grad):
    return (grad,)

def back_keep(v):
    return (v, None)

def back_low(kept, grad):
    return (low(grad),)
low.defvjp(low_keep, low_pass)
low_back.defvjp(back_keep, back_low)

def matmul(left, right):
    return jnp.dot(left, right, precision=HIGHEST)

def layer_norm(values):
    center = values - lax.optimization_barrier(jnp.mean(values, axis=-1, keepdims=True))
    return center * lax.rsqrt(lax.optimization_barrier(jnp.mean(center * center, axis=-1, keepdims=True)) + 1e-06)

def attend(query, keys, values):
    scores = low_back(jnp.einsum('qhd,khd->hqk', query, keys, precision=HIGHEST) * HD ** (-0.5))
    weights = low(jax.nn.softmax(scores, axis=-1))
    return low_back(low(jnp.einsum('hqk,khd->qhd', weights, values, precision=HIGHEST)))

def layer_block(x_lat, t_lat, e_lat, shift_table, q_weight, k_weight, v_weight, q_bias, v_bias, o_weight, o_bias, cq_weight, cq_bias, ck_weight, cv_weight, cv_bias, co_weight, co_bias, up_weight, up_bias, down_weight, down_bias):
    modulation = shift_table + e_lat
    first_normed = layer_norm(x_lat)
    first_hidden = low(first_normed * (1.0 + modulation[1]) + modulation[0])
    query = low_back(low(matmul(first_hidden, q_weight) + q_bias)).reshape(SEQ, HEADS, HD)
    keys = low_back(low(matmul(first_hidden, k_weight))).reshape(SEQ, HEADS, HD)
    values = low_back(low(matmul(first_hidden, v_weight) + v_bias)).reshape(SEQ, HEADS, HD)
    attended = attend(query, keys, values).reshape(SEQ, D)
    attention_result = low_back(matmul(attended, o_weight) + o_bias)
    first_residual = x_lat + modulation[2] * attention_result
    cross_in = low(first_residual)
    cross_query = low_back(low(matmul(cross_in, cq_weight) + cq_bias)).reshape(SEQ, HEADS, HD)
    text_keys = low_back(low(matmul(t_lat, ck_weight))).reshape(TXT, HEADS, HD)
    text_values = low_back(low(matmul(t_lat, cv_weight) + cv_bias)).reshape(TXT, HEADS, HD)
    cross_attended = attend(cross_query, text_keys, text_values).reshape(SEQ, D)
    cross_out = low_back(matmul(cross_attended, co_weight) + co_bias)
    x_two = first_residual + cross_out
    h_two = low(layer_norm(x_two) * (1.0 + modulation[4]) + modulation[3])
    pre_act = low_back(matmul(h_two, up_weight) + up_bias)
    hidden = low(jax.nn.gelu(pre_act, approximate=True))
    mlp_out = low_back(matmul(hidden, down_weight) + down_bias)
    return x_two + modulation[5] * mlp_out

def reference(latents_in, text_emb, time_emb, shift_table, q_weight, k_weight, v_weight, q_bias, v_bias, o_weight, o_bias, cq_weight, cq_bias, ck_weight, cv_weight, cv_bias, co_weight, co_bias, up_weight, up_bias, down_weight, down_bias, cotangent):
    params = tuple((p.astype(jnp.float32) for p in (shift_table, q_weight, k_weight, v_weight, q_bias, v_bias, o_weight, o_bias, cq_weight, cq_bias, ck_weight, cv_weight, cv_bias, co_weight, co_bias, up_weight, up_bias, down_weight, down_bias)))
    series = (latents_in.astype(jnp.float32).reshape(LATENTS, SEQ, D), text_emb.astype(jnp.float32).reshape(LATENTS, TXT, D), time_emb.astype(jnp.float32), cotangent.astype(jnp.float32).reshape(LATENTS, SEQ, D))

    def one_latent(carried, latent_item):
        x_lat, t_lat, e_lat, g_lat = latent_item
        layer_value, pullback = jax.vjp(layer_block, x_lat, t_lat, e_lat, *params)
        gradients = pullback(g_lat)
        carried = tuple((c + g for c, g in zip(carried, gradients[3:])))
        return (carried, (layer_value.astype(jnp.bfloat16), gradients[0], gradients[1], gradients[2]))
    zeros_init = tuple((jnp.zeros(p.shape, jnp.float32) for p in params))
    totals, stacked = lax.scan(one_latent, zeros_init, series)
    return (stacked[0].reshape(TOKENS, D), stacked[1].reshape(TOKENS, D), stacked[2].reshape(TEXT_ROWS, D), stacked[3], totals[0], totals[1], totals[2], totals[3], totals[4], totals[5], totals[6], totals[7], totals[8], totals[9], totals[10], totals[11], totals[12], totals[13], totals[14], totals[15], totals[16], totals[17], totals[18])
```

```python
import jax
import jax.numpy as jnp
from jax import lax
from jax.experimental import pallas as pl
from jax.experimental.pallas import tpu as pltpu
from jax.sharding import PartitionSpec as P


D = 1152
HD = 72
FLOAT = jnp.float32
HALF = jnp.bfloat16
EPSILON = 1e-06
SCALE = HD ** (-0.5)
VMEM_BYTES = 48 * 1024 * 1024

CORE = [(i, i ^ 1) for i in range(4)]
ACROSS = [(i, i ^ 2) for i in range(4)]
SWAP = [(0, 1), (1, 0)]


def place(x, k, y):
    return (x * 2 + k) * 2 + y


POINTS = [(x, k, y) for x in range(2) for k in range(2) for y in range(2)]
TURN = [(place(x, k, y), place(y, k, x)) for x, k, y in POINTS]
TURN_IN = [(place(x, k, y), place(1 - y, k, x)) for x, k, y in POINTS]
TURN_OUT = [(place(x, k, y), place(y, k, 1 - x)) for x, k, y in POINTS]


def to_core(value):
    return lax.ppermute(value, "row", CORE)


def to_x(value):
    return lax.ppermute(value, "row", ACROSS)


def to_y(value):
    return lax.ppermute(value, "col", SWAP)


def tie(*values):
    return lax.optimization_barrier(values)


def dot(left, right):
    return jnp.dot(left, right, preferred_element_type=FLOAT)


def lead_dot(left, right):
    return lax.dot_general(left, right, (((0,), (0,)), ((), ())), preferred_element_type=FLOAT)


def tail_dot(left, right):
    return lax.dot_general(left, right, (((1,), (1,)), ((), ())), preferred_element_type=FLOAT)


def cat(parts, axis):
    return jnp.concatenate(parts, axis)


def half(value):
    return value.astype(HALF)


def wide(value):
    return value.astype(FLOAT)


def tokens_sent(value, y):
    mid = value.shape[0] // 2
    low, high = value[:mid], value[mid:]
    first = lax.ppermute(jnp.where(y == 0, low, high), ("row", "col"), TURN)
    return first, lax.ppermute(jnp.where(y == 0, high, low), ("row", "col"), TURN_IN)


def tokens_got(first, second, same):
    return cat((jnp.where(same, first, second), jnp.where(same, second, first)), 1)


def halves_sent(pair, same):
    mid = pair.shape[1] // 2
    low, high = pair[:, :mid], pair[:, mid:]
    first = lax.ppermute(jnp.where(same, low, high), ("row", "col"), TURN)
    return first, lax.ppermute(jnp.where(same, high, low), ("row", "col"), TURN_OUT)


def halves_got(first, second, y):
    return cat((jnp.where(y == 0, first, second), jnp.where(y == 0, second, first)), 0)


def pair_mean(pair):
    return (jnp.sum(pair[0], 1, keepdims=True) + jnp.sum(pair[1], 1, keepdims=True)) / D


def layer_norm(pair):
    average = pair_mean(pair)
    center = [v - average for v in pair]
    inv_std = lax.rsqrt(pair_mean([c * c for c in center]) + EPSILON)
    return [c * inv_std for c in center], inv_std


def layer_norm_back(grad, normed, inv_std):
    average = pair_mean(grad)
    crossed = pair_mean([g * n for g, n in zip(grad, normed)])
    return [inv_std * (g - average - n * crossed) for g, n in zip(grad, normed)]


def row_sum(value):
    return jnp.sum(value, 0, keepdims=True)


def gelu(v):
    return 0.5 * v * (1.0 + jnp.tanh(0.7978845608028654 * (v + 0.044715 * v * v * v)))


def gelu_slope(v):
    t = jnp.tanh(0.7978845608028654 * (v + 0.044715 * v * v * v))
    return 0.5 * (1.0 + t) + 0.5 * v * (1.0 - t * t) * 0.7978845608028654 * (
        1.0 + 3.0 * 0.044715 * v * v
    )


def call(kernel, outs, args, scratch=(), smem=()):
    vmem = pl.BlockSpec(memory_space=pltpu.VMEM)
    specs = [pl.BlockSpec(memory_space=pltpu.SMEM) if i in smem else vmem for i in range(len(args))]
    return pl.pallas_call(
        kernel,
        out_shape=outs,
        in_specs=specs,
        out_specs=[vmem] * len(outs),
        scratch_shapes=scratch,
        compiler_params=pltpu.CompilerParams(vmem_limit_bytes=VMEM_BYTES),
        cost_estimate=pl.CostEstimate(flops=1, bytes_accessed=1, transcendentals=0),
    )(*args)


class Pair:
    def __init__(self, ref, count=2):
        self.ref, self.size, self.rows = ref, ref.shape[1] // count, ref.shape[0]

    def __getitem__(self, i):
        return self.ref[:, pl.ds(i * self.size, self.size)]

    def __setitem__(self, i, value):
        self.ref[:, pl.ds(i * self.size, self.size)] = value


def shape(dims, dtype):
    return jax.ShapeDtypeStruct(dims, dtype)


def bias_kernel(first_col, own, got, out):
    quarter = own.shape[1] // 4
    low_own = first_col[0] == 1
    at = 0
    for r, begin, size in [(0, i * quarter, quarter) for i in range(4)] + [(1, 0, 4 * quarter)]:
        a, b = own[r : r + 1, pl.ds(begin, size)], got[r : r + 1, pl.ds(begin, size)]
        out[:, pl.ds(at, size)] = jnp.where(low_own, a, b)
        out[:, pl.ds(at + size, size)] = jnp.where(low_own, b, a)
        at += 2 * size


def norm_kernel(x_ref, mods, out):
    x_ref, out = Pair(x_ref), Pair(out)
    normed, _ = layer_norm([wide(x_ref[0]), wide(x_ref[1])])
    for i in range(2):
        out[i] = half(normed[i] * (1.0 + mods[i, 1:2, :]) + mods[i, 0:1, :])


def project_kernel(near, far, own_m, got_m, own_s, got_s, row_m, row_s, q_out, kv_out):
    near, far = Pair(near), Pair(far)
    own_m, got_m, own_s, got_s = (Pair(w, 3) for w in (own_m, got_m, own_s, got_s))
    block = own_m.rows
    rows = near.rows
    for part in range(2):
        a, b = (near, far)[part][0], (near, far)[part][1]
        at = pl.ds(part * rows, rows)
        for i in range(3):
            for j in range(2):
                own, got = ((own_m, got_m), (own_s, got_s))[j]
                bias = (row_m, row_s)[j]
                out = tail_dot(a, own[i]) + tail_dot(b, got[i])
                if i == 0:
                    q_out[at, pl.ds(j * block, block)] = half(out + bias[:, :block])
                else:
                    if i == 2:
                        out = out + bias[:, block : 2 * block]
                    kv_out[at, pl.ds(((i - 1) * 2 + j) * block, block)] = half(out)


def attend_head(q, k, v):
    scores = tail_dot(k, q) * SCALE
    peak = jnp.max(scores, 0, keepdims=True)
    raised = jnp.exp(scores - peak)
    summed = jnp.sum(raised, 0, keepdims=True)
    mixed = dot(v.T, half(raised)) / summed
    return half(mixed.T), peak + jnp.log(summed)


def attend_head_back(q, k, v, g, lse):
    prob = jnp.exp(tail_dot(k, q) * SCALE - lse)
    grad_prob = tail_dot(v, g)
    centre = jnp.sum(prob * grad_prob, 0, keepdims=True)
    grad_score = half(prob * (grad_prob - centre))
    grad_q = (dot(k.T, grad_score) * SCALE).T
    grad_k = dot(grad_score, q) * SCALE
    grad_v = dot(half(prob), g)
    return grad_q, grad_k, grad_v


def attend_kernel(q_ref, near, far, out_ref, lse_ref):
    heads = q_ref.shape[1] // HD
    width = heads * HD
    for h in range(heads):
        at = pl.ds(h * HD, HD)
        there = (h + heads // 2) % heads * HD
        k = cat((near[:, at], far[:, pl.ds(there, HD)]), 0)
        v = cat((near[:, pl.ds(width + h * HD, HD)], far[:, pl.ds(width + there, HD)]), 0)
        for c in range(2):
            rows = pl.ds(c * (q_ref.shape[0] // 2), q_ref.shape[0] // 2)
            mixed, lse = attend_head(q_ref[rows, at], k, v)
            out_ref[rows, at] = mixed
            lse_ref[pl.ds(h, 1), rows] = lse


def attend_back_kernel(q_ref, near, far, lse_ref, g_ref, gq_ref, keep_ref, send_ref):
    heads = q_ref.shape[1] // HD
    width = heads * HD
    tokens = near.shape[0]
    for h in range(heads):
        at = pl.ds(h * HD, HD)
        there = (h + heads // 2) % heads * HD
        k = cat((near[:, at], far[:, pl.ds(there, HD)]), 0)
        v = cat((near[:, pl.ds(width + h * HD, HD)], far[:, pl.ds(width + there, HD)]), 0)
        total_k, total_v = None, None
        for c in range(2):
            rows = pl.ds(c * (q_ref.shape[0] // 2), q_ref.shape[0] // 2)
            gq, gk, gv = attend_head_back(
                q_ref[rows, at], k, v, g_ref[rows, at], lse_ref[pl.ds(h, 1), rows]
            )
            gq_ref[rows, at] = half(gq)
            total_k = gk if total_k is None else total_k + gk
            total_v = gv if total_v is None else total_v + gv
        keep_ref[:, at] = total_k[:tokens]
        keep_ref[:, pl.ds(width + h * HD, HD)] = total_v[:tokens]
        send_ref[:, pl.ds(there, HD)] = half(total_k[tokens:])
        send_ref[:, pl.ds(width + there, HD)] = half(total_v[tokens:])


def out_kernel(att, own_m, got_m, own_s, got_s, near, far):
    near, far = Pair(near), Pair(far)
    block = own_m.shape[0]
    rows = near.rows
    for part in range(2):
        at = pl.ds(part * rows, rows)
        a, b = att[at, :block], att[at, pl.ds(block, block)]
        for i in range(2):
            w_m, w_s = ((own_m, own_s), (got_m, got_s))[i]
            out = dot(a, w_m[...]) + dot(b, w_s[...])
            if part == 0:
                near[i] = out
            else:
                far[i] = half(out)


def out_back_kernel(near, far, att, own_m, got_m, own_s, got_s, grad_att, keep, send):
    near, far, keep, send = Pair(near), Pair(far), Pair(keep), Pair(send)
    block = own_m.shape[0]
    rows = near.rows
    for part in range(2):
        at = pl.ds(part * rows, rows)
        a, b = (near, far)[part][0], (near, far)[part][1]
        for j in range(2):
            own, got = ((own_m, got_m), (own_s, got_s))[j]
            grad_att[at, pl.ds(j * block, block)] = half(tail_dot(a, own[...]) + tail_dot(b, got[...]))
    for j in range(2):
        a = att[:rows, pl.ds(j * block, block)]
        b = att[rows:, pl.ds(j * block, block)]
        for i in range(2):
            (keep, send)[j][i] = half(lead_dot(a, near[i]) + lead_dot(b, far[i]))


def cross_kernel(x_ref, mods, near, far, row_m, row_s, far_bias, text_near, text_far, *refs):
    weights = [Pair(w) for w in refs[:8]]
    x_ref, near, far = Pair(x_ref), Pair(near), Pair(far)
    attn_out, cross_in, q_out, att_out, lse_ref, two_ref, h_ref = refs[8:]
    attn_out, cross_in, two_ref, h_ref = (Pair(v) for v in (attn_out, cross_in, two_ref, h_ref))
    block = weights[0].rows
    for i in range(2):
        attn = near[i] + wide(far[i]) + mods[i, 6:7, :]
        attn_out[i] = attn
        one = wide(x_ref[i]) + mods[i, 2:3, :] * attn
        cross_in[i] = half(one)
        two_ref[i] = one + mods[i, 7:8, :]
    a, b = cross_in[0], cross_in[1]
    for n in range(4):
        pair = weights[2 * n], weights[2 * n + 1]
        bias = (row_m, row_s)[n][:, 2 * block : 3 * block] if n < 2 else far_bias[:, (n - 2) * block : (n - 1) * block]
        q_out[n] = half(tail_dot(a, pair[0][0]) + tail_dot(b, pair[1][0]) + bias)
        text = (text_near, text_far)[n // 2]
        base = (n % 2) * 2 * block
        for h in range(block // HD):
            at = pl.ds(h * HD, HD)
            mixed, lse = attend_head(
                q_out[n, :, at],
                text[:, pl.ds(base + h * HD, HD)],
                text[:, pl.ds(base + block + h * HD, HD)],
            )
            att_out[n, :, at] = mixed
            lse_ref[pl.ds(n * (block // HD) + h, 1), :] = lse
        att = att_out[n]
        for i in range(2):
            two_ref[i] += dot(att, pair[i][1])
    normed, _ = layer_norm([two_ref[0], two_ref[1]])
    for i in range(2):
        h_ref[i] = half(normed[i] * (1.0 + mods[i, 4:5, :]) + mods[i, 3:4, :])


def cross_back_kernel(g_ref, mods, two_ref, near, far, attn_out, q_ref, lse_ref, text_near, text_far, *refs):
    weights = [Pair(w) for w in refs[:8]]
    g_ref, two_ref, near, far, attn_out = (Pair(v) for v in (g_ref, two_ref, near, far, attn_out))
    grad_cross, gq_out, near_out, far_out, one_ref, grad_attn, sums, grad_scratch = refs[8:]
    grad_cross, one_ref, grad_attn = Pair(grad_cross), Pair(one_ref), Pair(grad_attn)
    block = weights[0].rows
    normed, inv_std = layer_norm([two_ref[0], two_ref[1]])
    grads = [near[i] + wide(far[i]) for i in range(2)]
    back = layer_norm_back([grads[i] * (1.0 + mods[i, 4:5, :]) for i in range(2)], normed, inv_std)
    for i in range(2):
        sums[i, 0:1, :] = row_sum(grads[i])
        sums[i, 1:2, :] = row_sum(grads[i] * normed[i])
        grad = wide(g_ref[i]) + back[i]
        one_ref[i] = grad
        grad_cross[i] = half(grad)
        sums[i, 2:3, :] = row_sum(wide(half(grad)))
    a, b = grad_cross[0], grad_cross[1]
    for n in range(4):
        pair = weights[2 * n], weights[2 * n + 1]
        grad_scratch[...] = half(tail_dot(a, pair[0][1]) + tail_dot(b, pair[1][1]))
        text, text_out = ((text_near, near_out), (text_far, far_out))[n // 2]
        base = (n % 2) * 2 * block
        for h in range(block // HD):
            at = pl.ds(h * HD, HD)
            k_at, v_at = pl.ds(base + h * HD, HD), pl.ds(base + block + h * HD, HD)
            gq, gk, gv = attend_head_back(
                q_ref[n, :, at],
                text[:, k_at],
                text[:, v_at],
                grad_scratch[:, at],
                lse_ref[pl.ds(n * (block // HD) + h, 1), :],
            )
            gq_out[n, :, at] = half(gq)
            text_out[:, k_at] = half(gk)
            text_out[:, v_at] = half(gv)
        gq = gq_out[n]
        for i in range(2):
            one_ref[i] += dot(gq, pair[i][0])
    for i in range(2):
        one = one_ref[i]
        attn = half(one * mods[i, 2:3, :])
        grad_attn[i] = attn
        sums[i, 3:4, :] = row_sum(one * attn_out[i])
        sums[i, 4:5, :] = row_sum(wide(attn))


def cross_weight_kernel(x_ref, g_ref, q_ref, att_ref, keep_m, keep_x, send_m, send_x):
    x_ref, g_ref = Pair(x_ref), Pair(g_ref)
    for n, out in enumerate((keep_m, send_m, keep_x, send_x)):
        out = Pair(out, 4)
        for i in range(2):
            out[2 * i] = half(lead_dot(q_ref[n], x_ref[i]))
            out[2 * i + 1] = half(lead_dot(att_ref[n], g_ref[i]))


def rest_kernel(cqo, cqo_got, text_near, text_got, text_own, text_other, ckv_own, ckv_got, o_ref, o_got, *refs):
    outs, (grad_text, text_part, cv_sum) = refs[:2], refs[2:]
    cqo, cqo_got, o_ref, o_got, text_part = (
        Pair(cqo, 4), Pair(cqo_got, 4), Pair(o_ref), Pair(o_got), Pair(text_part)
    )
    grad_text[...] = half(wide(text_near[...]) + wide(text_got[...]))
    block = cqo.rows
    gk, gv = grad_text[:, :block], grad_text[:, pl.ds(block, block)]
    cv_sum[...] = row_sum(wide(gv))
    for i in range(2):
        out, text, weight = Pair(outs[i], 5), (text_own, text_other)[i], Pair((ckv_own, ckv_got)[i])
        for n in range(2):
            out[n] = half(wide(cqo[2 * i + n]) + wide(cqo_got[2 * i + n]))
        out[2] = half(lead_dot(gk, text[...]))
        out[3] = half(lead_dot(gv, text[...]))
        out[4] = half(wide(o_ref[i]) + wide(o_got[i]))
        text_part[i] = half(dot(gk, weight[0]) + dot(gv, weight[1]))


def up_kernel(near, far, own_m, got_m, own_s, got_s, row_m, row_s, pre, hidden):
    near, far = Pair(near), Pair(far)
    rows, ff = near.rows, own_m.shape[1]
    for part in range(2):
        a, b = (near, far)[part][0], (near, far)[part][1]
        at = pl.ds(part * rows, rows)
        for j in range(2):
            own, got = ((own_m, got_m), (own_s, got_s))[j]
            bias = (row_m, row_s)[j]
            out = dot(a, own[...]) + dot(b, got[...]) + bias[:, pl.ds(bias.shape[1] - ff, ff)]
            pre[j, at, :] = out
            hidden[j, at, :] = half(gelu(out))


def mlp_back_kernel(g_near, g_far, pre, *refs):
    g_near, g_far = Pair(g_near), Pair(g_far)
    up, down, (grad_pre, near, far, sums) = refs[:4], refs[4:8], refs[8:]
    near, far = Pair(near), Pair(far)
    rows = near.rows
    total = [None, None]
    for part in range(2):
        a, b = (g_near, g_far)[part][0], (g_near, g_far)[part][1]
        at = pl.ds(part * rows, rows)
        for j in range(2):
            grad = dot(a, down[2 * j][...]) + dot(b, down[2 * j + 1][...])
            grad = half(grad * gelu_slope(pre[j, at, :]))
            grad_pre[j, at, :] = grad
            term = row_sum(wide(grad))
            total[j] = term if part == 0 else total[j] + term
        for i in range(2):
            out = tail_dot(grad_pre[0, at, :], up[i][...]) + tail_dot(grad_pre[1, at, :], up[2 + i][...])
            if part == 0:
                near[i] = out
            else:
                far[i] = half(out)
    sums[0:1, :] = total[0]
    sums[1:2, :] = total[1]


def ff_weight_kernel(near, far, ff, keep0, keep1, send0, send1):
    near, far = Pair(near), Pair(far)
    rows = near.rows
    for j in range(2):
        for i in range(2):
            out = lead_dot(near[i], ff[j, :rows, :]) + lead_dot(far[i], ff[j, rows:, :])
            ((keep0, keep1), (send0, send1))[j][i][...] = half(out)


def down_kernel(hidden, own_m, got_m, own_s, got_s, near, far):
    near, far = Pair(near), Pair(far)
    rows = near.rows
    for part in range(2):
        at = pl.ds(part * rows, rows)
        for i in range(2):
            w_m, w_s = ((own_m, own_s), (got_m, got_s))[i]
            out = tail_dot(hidden[0, at, :], w_m[...]) + tail_dot(hidden[1, at, :], w_s[...])
            if part == 0:
                near[i] = out
            else:
                far[i] = half(out)


def layer_out_kernel(near, far, two_ref, mods, g_ref, gm_ref, out, sums):
    near, far, two_ref, g_ref, gm_ref, out = (Pair(v) for v in (near, far, two_ref, g_ref, gm_ref, out))
    for i in range(2):
        mlp_out = near[i] + wide(far[i]) + mods[i, 8:9, :]
        out[i] = half(two_ref[i] + mods[i, 5:6, :] * mlp_out)
        sums[i, 0:1, :] = row_sum(wide(g_ref[i]) * mlp_out)
        sums[i, 1:2, :] = row_sum(wide(gm_ref[i]))


def project_back_kernel(gq, keep, got, own_m, got_m, own_s, got_s, near, far, grad_m, grad_s, sums):
    near, far = Pair(near), Pair(far)
    own_m, got_m, own_s, got_s = (Pair(w, 3) for w in (own_m, got_m, own_s, got_s))
    block = own_m.rows
    rows = near.rows
    for part in range(2):
        at = pl.ds(part * rows, rows)
        total = [None, None]
        for i in range(3):
            for j in range(2):
                if i == 0:
                    g = gq[at, pl.ds(j * block, block)]
                else:
                    lanes = pl.ds(((i - 1) * 2 + j) * block, block)
                    g = half(keep[at, lanes] + wide(got[at, lanes]))
                (grad_m, grad_s)[j][at, pl.ds(i * block, block)] = g
                for n in range(2):
                    w = ((own_m, got_m), (own_s, got_s))[j][n]
                    term = dot(g, w[i])
                    total[n] = term if total[n] is None else total[n] + term
        for n in range(2):
            if part == 0:
                near[n] = total[n]
            else:
                far[n] = half(total[n])
    sums[0:1, :] = row_sum(wide(grad_m[...]))
    sums[1:2, :] = row_sum(wide(grad_s[...]))


def project_weight_kernel(near, far, grad_m, grad_s, keep0, keep1, send0, send1):
    near, far = Pair(near), Pair(far)
    rows = near.rows
    for j in range(2):
        grad = (grad_m, grad_s)[j]
        block = grad.shape[1] // 3
        for i in range(2):
            out = Pair(((keep0, keep1), (send0, send1))[j][i], 3)
            for n in range(3):
                g_near = grad[:rows, pl.ds(n * block, block)]
                g_far = grad[rows:, pl.ds(n * block, block)]
                out[n] = half(lead_dot(g_near, near[i]) + lead_dot(g_far, far[i]))


def norm_back_kernel(x_ref, mods, near, far, one_ref, out, sums):
    x_ref, near, far, one_ref, out = (Pair(v) for v in (x_ref, near, far, one_ref, out))
    normed, inv_std = layer_norm([wide(x_ref[0]), wide(x_ref[1])])
    grads = [near[i] + wide(far[i]) for i in range(2)]
    back = layer_norm_back([grads[i] * (1.0 + mods[i, 1:2, :]) for i in range(2)], normed, inv_std)
    for i in range(2):
        out[i] = half(one_ref[i] + back[i])
        sums[i, 0:1, :] = row_sum(grads[i])
        sums[i, 1:2, :] = row_sum(grads[i] * normed[i])


def dp_pairs(step):
    return [(i, i ^ step) for i in range(lax.axis_size("dp"))]


def by_halves(value):
    count = lax.axis_size("dp")
    return count & (count - 1) == 0 and value.shape[0] % count == 0


def dp_steps():
    return [1 << i for i in range(lax.axis_size("dp").bit_length() - 1)]


def reduce_sent(value, step):
    mid = value.shape[0] // 2
    upper = (lax.axis_index("dp") & step) != 0
    low, high = value[:mid], value[mid:]
    got = lax.ppermute(jnp.where(upper, low, high), "dp", dp_pairs(step))
    return jnp.where(upper, high, low), got


def reduce_got(kept, got):
    return half(wide(kept) + wide(got))


def gather_sent(value, step):
    return value, lax.ppermute(value, "dp", dp_pairs(step))


def gather_got(value, got, step):
    upper = (lax.axis_index("dp") & step) != 0
    return cat((jnp.where(upper, got, value), jnp.where(upper, value, got)), 0)


class DpSum:
    def __init__(self, value):
        self.value, self.flying = value, ()
        if by_halves(value):
            self.todo = [(True, step) for step in dp_steps()]
            self.todo += [(False, step) for step in reversed(dp_steps())]
        else:
            self.todo = []
            self.value = lax.psum(value, "dp")

    def send(self):
        if self.todo:
            reduce, step = self.todo[0]
            self.flying = (reduce_sent if reduce else gather_sent)(self.value, step)

    def land(self):
        if self.flying:
            reduce, step = self.todo.pop(0)
            if reduce:
                self.value = reduce_got(*self.flying)
            else:
                self.value = gather_got(*self.flying, step)
            self.flying = ()

    def next(self):
        self.land()
        self.send()

    def finish(self):
        self.land()
        while self.todo:
            self.send()
            self.land()
        return self.value


def tie_sums(sums, *values):
    flying = [v for one in sums for v in one.flying]
    out = tie(*values, *flying)
    rest = list(out[len(values) :])
    for one in sums:
        one.flying = tuple(rest.pop(0) for _ in one.flying)
        one.land()
    return out[: len(values)]


def small_sum_over_dp(value):
    if lax.axis_size("dp") != 4:
        return lax.psum(value, "dp")
    return value + sum(lax.ppermute(value, "dp", dp_pairs(i)) for i in range(1, 4))


def on_device(
    latents_in,
    text_emb,
    time_emb,
    shift_table,
    q_weight,
    k_weight,
    v_weight,
    q_bias,
    v_bias,
    o_weight,
    o_bias,
    cq_weight,
    cq_bias,
    ck_weight,
    cv_weight,
    cv_bias,
    co_weight,
    co_bias,
    up_weight,
    up_bias,
    down_weight,
    down_bias,
    cotangent,
):
    row = lax.axis_index("row")
    y = lax.axis_index("col")
    same = row // 2 == y
    first_col = y == 0
    part = D // 2
    text_rows = text_emb.shape[0] // 2
    block = q_weight.shape[1]
    quarter = block // 2
    ff = up_weight.shape[1]
    own = latents_in.shape[0] // 2
    tokens = 2 * own
    pair_wide, pair_half = shape((own, D), FLOAT), shape((own, D), HALF)

    def in_order(mine, other):
        return jnp.where(first_col, cat((mine, other), 0), cat((other, mine), 0))

    latents = tokens_got(*tokens_sent(latents_in, y), same)
    mods = wide(shift_table)[None] + wide(time_emb)
    row_own = cat((wide(cat((q_bias, v_bias, cq_bias, cv_bias), 0))[None], wide(up_bias)[None]), 0)
    out_bias = jnp.stack([wide(v) for v in (o_bias, co_bias, down_bias)])
    small_got = to_y(cat((jnp.where(first_col, mods[1], mods[0]), out_bias, row_own), 0))
    qkv_own, small_got = tie(cat((q_weight.T, k_weight.T, v_weight.T), 1), small_got)
    mods = jnp.stack((cat((jnp.where(first_col, mods[0], mods[1]), out_bias), 0), small_got[:9]))
    (row_m,) = call(
        bias_kernel,
        [shape((1, 4 * block + ff), FLOAT)],
        [first_col.astype(jnp.int32).reshape(1), row_own, small_got[9:]],
        smem=(0,),
    )
    row_s = to_core(row_m)

    qkv_got = to_y(qkv_own)
    qkv_core = to_core(qkv_own)
    o_core = to_core(o_weight)
    down_own = down_weight.T
    up_core, down_core = to_core(up_weight), to_core(down_own)
    text_own = jnp.where(first_col, text_emb[:text_rows], text_emb[text_rows:])
    text_sent = jnp.where(first_col, text_emb[text_rows:], text_emb[:text_rows])
    o_own, up_own = o_weight, up_weight
    cqo_own, ckv_own = cat((cq_weight.T, co_weight), 1), cat((ck_weight.T, cv_weight.T), 1)
    latents, cqo_own, ckv_own = tie(latents, cqo_own, ckv_own)
    o_got = to_y(o_own)
    cqo_got = to_y(cqo_own)
    (h_one,) = call(norm_kernel, [pair_half], [latents, mods])
    h_one_far = to_x(h_one)

    h_one_far, qkv_got, cqo_own, ckv_own = tie(h_one_far, qkv_got, cqo_own, ckv_own)
    cqo_x = to_x(cqo_own)
    ckv_got = to_y(ckv_own)
    text_got = to_y(text_sent)
    qkv = [qkv_own, qkv_got, qkv_core, to_core(qkv_got)]
    query, kv = call(
        project_kernel,
        [shape((tokens, 2 * block), HALF), shape((tokens, 4 * block), HALF)],
        [h_one, h_one_far] + qkv + [row_m, row_s],
    )
    kv_far = to_core(kv)
    up_got = to_y(up_own)
    attended, lse = call(
        attend_kernel,
        [shape((tokens, 2 * block), HALF), shape((2 * block // HD, tokens), FLOAT)],
        [query, kv, kv_far],
    )
    attended, o_got, cqo_x, cqo_got = tie(attended, o_got, cqo_x, cqo_got)
    cqo_got_x = to_x(cqo_got)
    outs = [o_own, o_got, o_core, to_core(o_got)]
    attn_near, attn_far = call(out_kernel, [pair_wide, pair_half], [attended] + outs)
    attn_far, ckv_got, text_got = tie(attn_far, ckv_got, text_got)
    attn_far = to_x(attn_far)
    gradient = tokens_sent(cotangent, y)
    down_got = to_y(down_own)

    text_two = cat(
        [
            tail_dot(text_own, ckv_own[:, i * part : (i + 1) * part])
            + tail_dot(text_got, ckv_got[:, i * part : (i + 1) * part])
            for i in range(2)
        ],
        1,
    )
    text_two = half(
        text_two + cat((jnp.zeros((1, block), FLOAT), row_m[:, 3 * block : 4 * block]), 1)
    )
    text_near = cat((text_two, to_core(text_two)), 1)
    cq_bias_row = half(cat((row_m[:, 2 * block : 3 * block], row_s[:, 2 * block : 3 * block]), 1))
    text_far = to_x(cat((text_near, cat((cq_bias_row, cq_bias_row), 1)), 0))
    attn_far, text_far, cqo_got_x = tie(attn_far, text_far, cqo_got_x)
    cqo_all = (
        cqo_own,
        cqo_got,
        to_core(cqo_own),
        to_core(cqo_got),
        cqo_x,
        cqo_got_x,
        to_core(cqo_x),
        to_core(cqo_got_x),
    )
    far_bias = wide(text_far[text_rows:, : 2 * block])
    text_far = text_far[:text_rows]

    attn_out, cross_in, cross_query, cross_att, cross_lse, x_two, h_two = call(
        cross_kernel,
        [
            pair_wide,
            pair_half,
            shape((4, own, block), HALF),
            shape((4, own, block), HALF),
            shape((D // HD, own), FLOAT),
            pair_wide,
            pair_half,
        ],
        [latents, mods, attn_near, attn_far, row_m, row_s, far_bias, text_near, text_far, *cqo_all],
    )

    h_two, up_got, *gradient = tie(h_two, up_got, *gradient)
    h_two_far = to_x(h_two)
    gradient = tokens_got(*gradient, same)
    grad_mlp = half(cat((mods[0, 5:6], mods[1, 5:6]), 1) * wide(gradient))
    h_two_far, grad_mlp = tie(h_two_far, grad_mlp)
    grad_mlp_far = to_x(grad_mlp)
    up = [up_own, up_got, up_core, to_core(up_got)]
    pre, hidden = call(
        up_kernel,
        [shape((2, tokens, ff), FLOAT), shape((2, tokens, ff), HALF)],
        [h_two, h_two_far] + up + [row_m, row_s],
    )
    hidden, grad_mlp_far, down_got = tie(hidden, grad_mlp_far, down_got)

    ff_shape = shape((part, ff), HALF)
    down_keep, down_keep1, down_send, down_send1 = call(
        ff_weight_kernel, [ff_shape] * 4, [grad_mlp, grad_mlp_far, hidden]
    )
    down_keep = half(wide(down_keep) + wide(to_core(down_send)))
    down_far = half(wide(down_keep1) + wide(to_core(down_send1)))
    down_far, down_keep, hidden = tie(down_far, down_keep, hidden)
    down_far = to_y(down_far)
    down = [down_own, down_got, down_core, to_core(down_got)]
    grad_pre, two_near, two_far, pre_sums = call(
        mlp_back_kernel,
        [shape((2, tokens, ff), HALF), pair_wide, pair_half, shape((2, ff), FLOAT)],
        [grad_mlp, grad_mlp_far, pre] + up + down,
    )
    two_far = to_x(two_far)
    up_keep, up_keep1, up_send, up_send1 = call(
        ff_weight_kernel, [ff_shape] * 4, [h_two, h_two_far, grad_pre]
    )
    mlp_near, mlp_far = call(down_kernel, [pair_wide, pair_half], [hidden] + down)
    up_send, up_send1, up_keep, up_keep1, down_far, mlp_far = tie(
        up_send, up_send1, up_keep, up_keep1, down_far, mlp_far
    )
    up_keep = half(wide(up_keep) + wide(to_core(up_send)))
    up_far = half(wide(up_keep1) + wide(to_core(up_send1)))
    two_far, up_far, up_keep = tie(two_far, up_far, up_keep)
    up_far = to_y(up_far)
    down_sum = DpSum(half(wide(down_keep) + wide(down_far)))
    down_sum.send()

    text_shape = shape((text_rows, 4 * block), HALF)
    grad_cross, grad_cq, text_grad_near, text_grad_far, grad_x_one, grad_attn, cross_sums = call(
        cross_back_kernel,
        [
            pair_half,
            shape((4, own, block), HALF),
            text_shape,
            text_shape,
            pair_wide,
            pair_half,
            shape((2, 5, part), FLOAT),
        ],
        [gradient, mods, x_two, two_near, two_far, attn_out, cross_query, cross_lse, text_near, text_far, *cqo_all],
        [pltpu.VMEM((own, block), HALF)],
    )
    (grad_attn,) = tie_sums([down_sum], grad_attn)
    grad_attn_far = to_x(grad_attn)
    down_sum.send()
    cqo_shape = shape((block, 2 * D), HALF)
    cqo_keep, cqo_keep_x, cqo_send, cqo_send_x = call(
        cross_weight_kernel, [cqo_shape] * 4, [cross_in, grad_cross, grad_cq, cross_att]
    )
    text_grad_core = to_core(cat((text_grad_near[:, 2 * block :], text_grad_far[:, 2 * block :]), 1))
    cqo_keep = half(wide(cqo_keep) + wide(to_core(cqo_send)))
    cqo_far = half(wide(cqo_keep_x) + wide(to_core(cqo_send_x)))
    text_chip = half(
        wide(cat((text_grad_near[:, : 2 * block], text_grad_far[:, : 2 * block]), 1))
        + wide(text_grad_core)
    )
    grad_attn_far, up_far, cqo_far, text_chip, mlp_far = tie_sums(
        [down_sum], grad_attn_far, up_far, cqo_far, text_chip, mlp_far
    )

    up_sum = DpSum(half(wide(up_keep) + wide(up_far)))
    up_sum.send()
    down_sum.send()
    cqo_far = to_x(cqo_far)
    text_from = to_x(text_chip[:, 2 * block :])
    o_shape = shape((block, D), HALF)
    grad_att, o_keep, o_send = call(
        out_back_kernel,
        [shape((tokens, 2 * block), HALF), o_shape, o_shape],
        [grad_attn, grad_attn_far, attended] + outs,
    )
    grad_att, cqo_far, text_from = tie(grad_att, cqo_far, text_from)
    rest_shape = shape((block, 5 * part), HALF)
    rest_keep, rest_far, grad_text, text_part, cv_sum = call(
        rest_kernel,
        [
            rest_shape,
            rest_shape,
            shape((text_rows, 2 * block), HALF),
            shape((text_rows, D), HALF),
            shape((1, block), FLOAT),
        ],
        [
            cqo_keep,
            cqo_far,
            text_chip[:, : 2 * block],
            text_from,
            text_own,
            text_got,
            ckv_own,
            ckv_got,
            o_keep,
            to_core(o_send),
        ],
    )
    rest_far, mlp_far, grad_att = tie(rest_far, mlp_far, grad_att)
    rest_far = to_y(rest_far)
    mlp_far = to_x(mlp_far)
    grad_query, kv_keep, kv_send = call(
        attend_back_kernel,
        [
            shape((tokens, 2 * block), HALF),
            shape((tokens, 4 * block), FLOAT),
            shape((tokens, 4 * block), HALF),
        ],
        [query, kv, kv_far, lse, grad_att],
    )
    grad_query, kv_keep, kv_send, mlp_far = tie_sums(
        [up_sum, down_sum], grad_query, kv_keep, kv_send, mlp_far
    )
    up_sum.send()
    down_sum.send()
    kv_got = to_core(kv_send)
    layer_pair, layer_sums = call(
        layer_out_kernel,
        [pair_half, shape((2, 2, part), FLOAT)],
        [mlp_near, mlp_far, x_two, mods, gradient, grad_mlp],
    )
    layer_pair = halves_sent(layer_pair, same)
    text_near = to_core(text_part)
    grad_shape = shape((tokens, 3 * block), HALF)
    near, far, grad_m, grad_s, qkv_sums = call(
        project_back_kernel,
        [pair_wide, pair_half, grad_shape, grad_shape, shape((2, 3 * block), FLOAT)],
        [grad_query, kv_keep, kv_got] + qkv,
    )
    far, text_near, rest_far, *layer_pair = tie(far, text_near, rest_far, *layer_pair)
    far = to_x(far)
    rest_sum = DpSum(half(wide(rest_keep) + wide(rest_far)))
    rest_sum.send()
    layer_out = halves_got(*layer_pair, y)
    text_sum = wide(text_part) + wide(text_near)
    text_got = to_x(half(text_sum))
    qkv_shape = shape((block, 3 * part), HALF)
    qkv_keep, qkv_keep1, qkv_send, qkv_send1 = call(
        project_weight_kernel, [qkv_shape] * 4, [h_one, h_one_far, grad_m, grad_s]
    )
    qkv_send, qkv_send1, qkv_keep, qkv_keep1, text_got = tie_sums(
        [up_sum, down_sum], qkv_send, qkv_send1, qkv_keep, qkv_keep1, text_got
    )
    up_sum.send()
    qkv_far = to_y(half(wide(qkv_keep1) + wide(to_core(qkv_send1))))
    qkv_keep = half(wide(qkv_keep) + wide(to_core(qkv_send)))
    text_sum = text_sum + wide(text_got)
    text_far = to_y(half(text_sum[:, part:]))
    far, text_far = tie_sums([rest_sum], far, text_far)
    rest_sum.send()
    text_grad = in_order(text_sum[:, :part], wide(text_far))
    token_pair, one_sums = call(
        norm_back_kernel,
        [pair_half, shape((2, 2, part), FLOAT)],
        [latents, mods, near, far, grad_x_one],
    )
    token_sent = halves_sent(token_pair, same)
    (qkv_far,) = tie_sums([rest_sum, up_sum], qkv_far)
    qkv_sum = DpSum(half(wide(qkv_keep) + wide(qkv_far)))
    qkv_sum.send()
    rest_sum.send()
    up_sum.send()
    token_input_gradient = wide(halves_got(*token_sent, y))

    feature_sums = cat((one_sums, cross_sums, layer_sums), 1)
    flat = feature_sums.reshape(9 * D)
    gcq_sum = jnp.sum(wide(grad_cq), 1)
    cv_sum = cv_sum[0]
    core_got = to_core(
        cat((flat, gcq_sum[3], gcq_sum[1], qkv_sums[1, :block], qkv_sums[1, 2 * block :], pre_sums[1]), 0)
    )
    chip = core_got + cat(
        (flat, gcq_sum[2], gcq_sum[0], qkv_sums[0, :block], qkv_sums[0, 2 * block :], pre_sums[0]), 0
    )
    x_got = to_x(chip[: 9 * D + block])
    sums = (chip[: 9 * D] + x_got[: 9 * D]).reshape(2, 9, part)
    cq_row = chip[9 * D + block : 9 * D + 2 * block] + x_got[9 * D :]
    rest = chip[9 * D + 2 * block :]
    row_rows = [
        (v[: v.shape[0] // 2], v[v.shape[0] // 2 :])
        for v in (rest[:block], rest[block : 2 * block], cq_row, cv_sum, rest[2 * block :])
    ]
    row_low = cat([v[0] for v in row_rows], 0)
    row_high = cat([v[1] for v in row_rows], 0)
    row_mine = jnp.where(first_col, row_low, row_high)
    row_sent = jnp.where(first_col, row_high, row_low)
    col_got = to_y(cat((sums[1].reshape(9 * part), row_sent), 0))
    sums_got = col_got[: 9 * part].reshape(9, part)
    sums_own = sums[0]

    def six(v):
        return jnp.stack((v[0], v[1], v[5], v[2], v[3], v[7]))

    time_own, time_got = six(sums_own), six(sums_got)
    time_grad = jnp.where(first_col, jnp.stack((time_own, time_got)), jnp.stack((time_got, time_own)))
    totals = small_sum_over_dp(
        cat(((sums_own + sums_got).reshape(9 * part), row_mine + col_got[9 * part :]), 0)
    )
    table_grad = six(totals[: 9 * part].reshape(9, part))
    o_bias_grad, co_bias_grad, down_bias_grad = (
        totals[i * part : (i + 1) * part] for i in (6, 4, 8)
    )
    rows = totals[9 * part :]
    q_bias_grad, v_bias_grad, cq_bias_grad, cv_bias_grad = (
        rows[i * quarter : (i + 1) * quarter] for i in range(4)
    )
    up_bias_grad = rows[4 * quarter :]

    qkv_grad, rest_sum = qkv_sum.finish(), rest_sum.finish()
    up_sum, down_sum = up_sum.finish(), down_sum.finish()
    q_grad, k_grad, v_grad = (wide(qkv_grad[:, i * part : (i + 1) * part]).T for i in range(3))
    cq_grad, co_grad, ck_grad, cv_grad, o_grad = (
        wide(rest_sum[:, i * part : (i + 1) * part]) for i in range(5)
    )
    return (
        layer_out,
        token_input_gradient,
        text_grad,
        time_grad,
        table_grad,
        q_grad,
        k_grad,
        v_grad,
        q_bias_grad,
        v_bias_grad,
        o_grad,
        o_bias_grad,
        cq_grad.T,
        cq_bias_grad,
        ck_grad.T,
        cv_grad.T,
        cv_bias_grad,
        co_grad,
        co_bias_grad,
        wide(up_sum),
        up_bias_grad,
        wide(down_sum).T,
        down_bias_grad,
    )


def solution(mesh):
    in_specs = (
        P(("dp", "row"), "col"),
        P("dp", "col"),
        P("dp", None, "col"),
        P(None, "col"),
        P("col", "row"),
        P("col", "row"),
        P("col", "row"),
        P(("row", "col")),
        P(("row", "col")),
        P("row", "col"),
        P("col"),
        P("col", "row"),
        P(("row", "col")),
        P("col", "row"),
        P("col", "row"),
        P(("row", "col")),
        P("row", "col"),
        P("col"),
        P("col", "row"),
        P(("row", "col")),
        P("row", "col"),
        P("col"),
        P(("dp", "row"), "col"),
    )
    out_specs = (
        P(("dp", "row"), "col"),
        P(("dp", "row"), "col"),
        P("dp", "col"),
        P("dp", None, "col"),
        P(None, "col"),
        P("col", "row"),
        P("col", "row"),
        P("col", "row"),
        P(("row", "col")),
        P(("row", "col")),
        P("row", "col"),
        P("col"),
        P("col", "row"),
        P(("row", "col")),
        P("col", "row"),
        P("col", "row"),
        P(("row", "col")),
        P("row", "col"),
        P("col"),
        P("col", "row"),
        P(("row", "col")),
        P("row", "col"),
        P("col"),
    )
    return jax.shard_map(
        on_device, mesh=mesh, in_specs=in_specs, out_specs=out_specs, check_vma=False
    )
```

```python
import jax
import jax.numpy as jnp
from jax import lax
from jax.experimental import pallas as pl
from jax.experimental.pallas import tpu as pltpu
from jax.sharding import PartitionSpec as P


D = 1152
HD = 72
FLOAT = jnp.float32
HALF = jnp.bfloat16
EPSILON = 1e-06
SCALE = HD ** (-0.5)
VMEM_BYTES = 48 * 1024 * 1024

CORE = [(i, i ^ 1) for i in range(4)]
ACROSS = [(i, i ^ 2) for i in range(4)]
SWAP = [(0, 1), (1, 0)]


def place(x, k, y):
    return (x * 2 + k) * 2 + y


POINTS = [(x, k, y) for x in range(2) for k in range(2) for y in range(2)]
TURN = [(place(x, k, y), place(y, k, x)) for x, k, y in POINTS]
TURN_IN = [(place(x, k, y), place(1 - y, k, x)) for x, k, y in POINTS]
TURN_OUT = [(place(x, k, y), place(y, k, 1 - x)) for x, k, y in POINTS]


def to_core(value):
    return lax.ppermute(value, "row", CORE)


def to_x(value):
    return lax.ppermute(value, "row", ACROSS)


def to_y(value):
    return lax.ppermute(value, "col", SWAP)


def tie(*values):
    return lax.optimization_barrier(values)


def dot(left, right):
    return jnp.dot(left, right, preferred_element_type=FLOAT)


def lead_dot(left, right):
    return lax.dot_general(left, right, (((0,), (0,)), ((), ())), preferred_element_type=FLOAT)


def tail_dot(left, right):
    return lax.dot_general(left, right, (((1,), (1,)), ((), ())), preferred_element_type=FLOAT)


def cat(parts, axis):
    return jnp.concatenate(parts, axis)


def half(value):
    return value.astype(HALF)


def wide(value):
    return value.astype(FLOAT)


def tokens_sent(value, y):
    mid = value.shape[0] // 2
    low, high = value[:mid], value[mid:]
    first = lax.ppermute(jnp.where(y == 0, low, high), ("row", "col"), TURN)
    return first, lax.ppermute(jnp.where(y == 0, high, low), ("row", "col"), TURN_IN)


def tokens_got(first, second, same):
    return cat((jnp.where(same, first, second), jnp.where(same, second, first)), 1)


def halves_sent(pair, same):
    mid = pair.shape[1] // 2
    low, high = pair[:, :mid], pair[:, mid:]
    first = lax.ppermute(jnp.where(same, low, high), ("row", "col"), TURN)
    return first, lax.ppermute(jnp.where(same, high, low), ("row", "col"), TURN_OUT)


def halves_got(first, second, y):
    return cat((jnp.where(y == 0, first, second), jnp.where(y == 0, second, first)), 0)


def pair_mean(pair):
    return (jnp.sum(pair[0], 1, keepdims=True) + jnp.sum(pair[1], 1, keepdims=True)) / D


def layer_norm(pair):
    average = pair_mean(pair)
    center = [v - average for v in pair]
    inv_std = lax.rsqrt(pair_mean([c * c for c in center]) + EPSILON)
    return [c * inv_std for c in center], inv_std


def layer_norm_back(grad, normed, inv_std):
    average = pair_mean(grad)
    crossed = pair_mean([g * n for g, n in zip(grad, normed)])
    return [inv_std * (g - average - n * crossed) for g, n in zip(grad, normed)]


def row_sum(value):
    return jnp.sum(value, 0, keepdims=True)


def gelu(v):
    return 0.5 * v * (1.0 + jnp.tanh(0.7978845608028654 * (v + 0.044715 * v * v * v)))


def gelu_slope(v):
    t = jnp.tanh(0.7978845608028654 * (v + 0.044715 * v * v * v))
    return 0.5 * (1.0 + t) + 0.5 * v * (1.0 - t * t) * 0.7978845608028654 * (
        1.0 + 3.0 * 0.044715 * v * v
    )


def call(kernel, outs, args, scratch=(), smem=()):
    vmem = pl.BlockSpec(memory_space=pltpu.VMEM)
    specs = [pl.BlockSpec(memory_space=pltpu.SMEM) if i in smem else vmem for i in range(len(args))]
    return pl.pallas_call(
        kernel,
        out_shape=outs,
        in_specs=specs,
        out_specs=[vmem] * len(outs),
        scratch_shapes=scratch,
        compiler_params=pltpu.CompilerParams(vmem_limit_bytes=VMEM_BYTES),
        cost_estimate=pl.CostEstimate(flops=1, bytes_accessed=1, transcendentals=0),
    )(*args)


class Pair:
    def __init__(self, ref, count=2):
        self.ref, self.size, self.rows = ref, ref.shape[1] // count, ref.shape[0]

    def __getitem__(self, i):
        return self.ref[:, pl.ds(i * self.size, self.size)]

    def __setitem__(self, i, value):
        self.ref[:, pl.ds(i * self.size, self.size)] = value


def shape(dims, dtype):
    return jax.ShapeDtypeStruct(dims, dtype)


def bias_kernel(first_col, own, got, out):
    quarter = own.shape[1] // 4
    low_own = first_col[0] == 1
    at = 0
    for r, begin, size in [(0, i * quarter, quarter) for i in range(4)] + [(1, 0, 4 * quarter)]:
        a, b = own[r : r + 1, pl.ds(begin, size)], got[r : r + 1, pl.ds(begin, size)]
        out[:, pl.ds(at, size)] = jnp.where(low_own, a, b)
        out[:, pl.ds(at + size, size)] = jnp.where(low_own, b, a)
        at += 2 * size


def norm_kernel(x_ref, mods, out):
    x_ref, out = Pair(x_ref), Pair(out)
    normed, _ = layer_norm([wide(x_ref[0]), wide(x_ref[1])])
    for i in range(2):
        out[i] = half(normed[i] * (1.0 + mods[i, 1:2, :]) + mods[i, 0:1, :])


def project_kernel(near, far, own_m, got_m, own_s, got_s, row_m, row_s, q_out, kv_out):
    near, far = Pair(near), Pair(far)
    own_m, got_m, own_s, got_s = (Pair(w, 3) for w in (own_m, got_m, own_s, got_s))
    block = own_m.rows
    rows = near.rows
    for part in range(2):
        a, b = (near, far)[part][0], (near, far)[part][1]
        at = pl.ds(part * rows, rows)
        for i in range(3):
            for j in range(2):
                own, got = ((own_m, got_m), (own_s, got_s))[j]
                bias = (row_m, row_s)[j]
                out = tail_dot(a, own[i]) + tail_dot(b, got[i])
                if i == 0:
                    q_out[at, pl.ds(j * block, block)] = half(out + bias[:, :block])
                else:
                    if i == 2:
                        out = out + bias[:, block : 2 * block]
                    kv_out[at, pl.ds(((i - 1) * 2 + j) * block, block)] = half(out)


def attend_head(q, k, v):
    scores = tail_dot(k, q) * SCALE
    peak = jnp.max(scores, 0, keepdims=True)
    raised = jnp.exp(scores - peak)
    summed = jnp.sum(raised, 0, keepdims=True)
    mixed = dot(v.T, half(raised)) / summed
    return half(mixed.T), peak + jnp.log(summed)


def attend_head_back(q, k, v, g, lse):
    prob = jnp.exp(tail_dot(k, q) * SCALE - lse)
    grad_prob = tail_dot(v, g)
    centre = jnp.sum(prob * grad_prob, 0, keepdims=True)
    grad_score = half(prob * (grad_prob - centre))
    grad_q = (dot(k.T, grad_score) * SCALE).T
    grad_k = dot(grad_score, q) * SCALE
    grad_v = dot(half(prob), g)
    return grad_q, grad_k, grad_v


def attend_kernel(q_ref, near, far, out_ref, lse_ref):
    heads = q_ref.shape[1] // HD
    width = heads * HD
    for h in range(heads):
        at = pl.ds(h * HD, HD)
        there = (h + heads // 2) % heads * HD
        k = cat((near[:, at], far[:, pl.ds(there, HD)]), 0)
        v = cat((near[:, pl.ds(width + h * HD, HD)], far[:, pl.ds(width + there, HD)]), 0)
        for c in range(2):
            rows = pl.ds(c * (q_ref.shape[0] // 2), q_ref.shape[0] // 2)
            mixed, lse = attend_head(q_ref[rows, at], k, v)
            out_ref[rows, at] = mixed
            lse_ref[pl.ds(h, 1), rows] = lse


def attend_back_kernel(q_ref, near, far, lse_ref, g_ref, gq_ref, keep_ref, send_ref):
    heads = q_ref.shape[1] // HD
    width = heads * HD
    tokens = near.shape[0]
    for h in range(heads):
        at = pl.ds(h * HD, HD)
        there = (h + heads // 2) % heads * HD
        k = cat((near[:, at], far[:, pl.ds(there, HD)]), 0)
        v = cat((near[:, pl.ds(width + h * HD, HD)], far[:, pl.ds(width + there, HD)]), 0)
        total_k, total_v = None, None
        for c in range(2):
            rows = pl.ds(c * (q_ref.shape[0] // 2), q_ref.shape[0] // 2)
            gq, gk, gv = attend_head_back(
                q_ref[rows, at], k, v, g_ref[rows, at], lse_ref[pl.ds(h, 1), rows]
            )
            gq_ref[rows, at] = half(gq)
            total_k = gk if total_k is None else total_k + gk
            total_v = gv if total_v is None else total_v + gv
        keep_ref[:, at] = total_k[:tokens]
        keep_ref[:, pl.ds(width + h * HD, HD)] = total_v[:tokens]
        send_ref[:, pl.ds(there, HD)] = half(total_k[tokens:])
        send_ref[:, pl.ds(width + there, HD)] = half(total_v[tokens:])


def out_kernel(att, own_m, got_m, own_s, got_s, near, far):
    near, far = Pair(near), Pair(far)
    block = own_m.shape[0]
    rows = near.rows
    for part in range(2):
        at = pl.ds(part * rows, rows)
        a, b = att[at, :block], att[at, pl.ds(block, block)]
        for i in range(2):
            w_m, w_s = ((own_m, own_s), (got_m, got_s))[i]
            out = dot(a, w_m[...]) + dot(b, w_s[...])
            if part == 0:
                near[i] = out
            else:
                far[i] = half(out)


def out_back_kernel(near, far, att, own_m, got_m, own_s, got_s, grad_att, keep, send):
    near, far, keep, send = Pair(near), Pair(far), Pair(keep), Pair(send)
    block = own_m.shape[0]
    rows = near.rows
    for part in range(2):
        at = pl.ds(part * rows, rows)
        a, b = (near, far)[part][0], (near, far)[part][1]
        for j in range(2):
            own, got = ((own_m, got_m), (own_s, got_s))[j]
            grad_att[at, pl.ds(j * block, block)] = half(tail_dot(a, own[...]) + tail_dot(b, got[...]))
    for j in range(2):
        a = att[:rows, pl.ds(j * block, block)]
        b = att[rows:, pl.ds(j * block, block)]
        for i in range(2):
            (keep, send)[j][i] = half(lead_dot(a, near[i]) + lead_dot(b, far[i]))


def text_kernel(near, other, own, got, row_m, out):
    own, got = Pair(own), Pair(got)
    block = own.rows
    for i in range(2):
        sums = tail_dot(near[...], own[i]) + tail_dot(other[...], got[i])
        if i == 1:
            sums = sums + row_m[:, pl.ds(3 * block, block)]
        out[:, pl.ds(i * block, block)] = half(sums)


def cross_kernel(x_ref, mods, near, far, row_m, row_s, far_rows, text_near, text_far, *refs):
    weights = [Pair(w) for w in refs[:8]]
    x_ref, near, far = Pair(x_ref), Pair(near), Pair(far)
    attn_out, cross_in, q_out, att_out, lse_ref, two_ref, h_ref = refs[8:]
    attn_out, cross_in, two_ref, h_ref = (Pair(v) for v in (attn_out, cross_in, two_ref, h_ref))
    block = weights[0].rows
    for i in range(2):
        attn = near[i] + wide(far[i]) + mods[i, 6:7, :]
        attn_out[i] = attn
        one = wide(x_ref[i]) + mods[i, 2:3, :] * attn
        cross_in[i] = half(one)
        two_ref[i] = one + mods[i, 7:8, :]
    a, b = cross_in[0], cross_in[1]
    for n in range(4):
        pair = weights[2 * n], weights[2 * n + 1]
        bias = (row_m[...], row_s[...], far_rows[0:1, :], far_rows[1:2, :])[n]
        bias = bias[:, 2 * block : 3 * block]
        q_out[n] = half(tail_dot(a, pair[0][0]) + tail_dot(b, pair[1][0]) + bias)
        text = (text_near, text_far)[n // 2]
        base = (n % 2) * 2 * block
        for h in range(block // HD):
            at = pl.ds(h * HD, HD)
            mixed, lse = attend_head(
                q_out[n, :, at],
                text[:, pl.ds(base + h * HD, HD)],
                text[:, pl.ds(base + block + h * HD, HD)],
            )
            att_out[n, :, at] = mixed
            lse_ref[pl.ds(n * (block // HD) + h, 1), :] = lse
        att = att_out[n]
        for i in range(2):
            two_ref[i] += dot(att, pair[i][1])
    normed, _ = layer_norm([two_ref[0], two_ref[1]])
    for i in range(2):
        h_ref[i] = half(normed[i] * (1.0 + mods[i, 4:5, :]) + mods[i, 3:4, :])


def cross_back_kernel(g_ref, mods, two_ref, near, far, attn_out, q_ref, lse_ref, text_near, text_far, *refs):
    weights = [Pair(w) for w in refs[:8]]
    g_ref, two_ref, near, far, attn_out = (Pair(v) for v in (g_ref, two_ref, near, far, attn_out))
    grad_cross, gq_out, near_out, far_out, one_ref, grad_attn, sums, grad_scratch = refs[8:]
    grad_cross, one_ref, grad_attn = Pair(grad_cross), Pair(one_ref), Pair(grad_attn)
    block = weights[0].rows
    normed, inv_std = layer_norm([two_ref[0], two_ref[1]])
    grads = [near[i] + wide(far[i]) for i in range(2)]
    back = layer_norm_back([grads[i] * (1.0 + mods[i, 4:5, :]) for i in range(2)], normed, inv_std)
    for i in range(2):
        sums[i, 0:1, :] = row_sum(grads[i])
        sums[i, 1:2, :] = row_sum(grads[i] * normed[i])
        grad = wide(g_ref[i]) + back[i]
        one_ref[i] = grad
        grad_cross[i] = half(grad)
        sums[i, 2:3, :] = row_sum(wide(half(grad)))
    a, b = grad_cross[0], grad_cross[1]
    for n in range(4):
        pair = weights[2 * n], weights[2 * n + 1]
        grad_scratch[...] = half(tail_dot(a, pair[0][1]) + tail_dot(b, pair[1][1]))
        text, text_out = ((text_near, near_out), (text_far, far_out))[n // 2]
        base = (n % 2) * 2 * block
        for h in range(block // HD):
            at = pl.ds(h * HD, HD)
            k_at, v_at = pl.ds(base + h * HD, HD), pl.ds(base + block + h * HD, HD)
            gq, gk, gv = attend_head_back(
                q_ref[n, :, at],
                text[:, k_at],
                text[:, v_at],
                grad_scratch[:, at],
                lse_ref[pl.ds(n * (block // HD) + h, 1), :],
            )
            gq_out[n, :, at] = half(gq)
            text_out[:, k_at] = half(gk)
            text_out[:, v_at] = half(gv)
        gq = gq_out[n]
        for i in range(2):
            one_ref[i] += dot(gq, pair[i][0])
    for i in range(2):
        one = one_ref[i]
        attn = half(one * mods[i, 2:3, :])
        grad_attn[i] = attn
        sums[i, 3:4, :] = row_sum(one * attn_out[i])
        sums[i, 4:5, :] = row_sum(wide(attn))


def cross_weight_kernel(x_ref, g_ref, q_ref, att_ref, keep_m, keep_x, send_m, send_x):
    x_ref, g_ref = Pair(x_ref), Pair(g_ref)
    for n, out in enumerate((keep_m, send_m, keep_x, send_x)):
        out = Pair(out, 4)
        for i in range(2):
            out[2 * i] = half(lead_dot(q_ref[n], x_ref[i]))
            out[2 * i + 1] = half(lead_dot(att_ref[n], g_ref[i]))


def rest_kernel(cqo, cqo_got, text_near, text_got, text_own, text_other, ckv_own, ckv_got, o_ref, o_got, *refs):
    outs, (grad_text, text_part, cv_sum) = refs[:2], refs[2:]
    cqo, cqo_got, o_ref, o_got, text_part = (
        Pair(cqo, 4), Pair(cqo_got, 4), Pair(o_ref), Pair(o_got), Pair(text_part)
    )
    grad_text[...] = half(wide(text_near[...]) + wide(text_got[...]))
    block = cqo.rows
    gk, gv = grad_text[:, :block], grad_text[:, pl.ds(block, block)]
    cv_sum[...] = row_sum(wide(gv))
    for i in range(2):
        out, text, weight = Pair(outs[i], 5), (text_own, text_other)[i], Pair((ckv_own, ckv_got)[i])
        for n in range(2):
            out[n] = half(wide(cqo[2 * i + n]) + wide(cqo_got[2 * i + n]))
        out[2] = half(lead_dot(gk, text[...]))
        out[3] = half(lead_dot(gv, text[...]))
        out[4] = half(wide(o_ref[i]) + wide(o_got[i]))
        text_part[i] = half(dot(gk, weight[0]) + dot(gv, weight[1]))


def up_kernel(near, far, own_m, got_m, own_s, got_s, row_m, row_s, pre, hidden):
    near, far = Pair(near), Pair(far)
    rows, ff = near.rows, own_m.shape[1]
    for part in range(2):
        a, b = (near, far)[part][0], (near, far)[part][1]
        at = pl.ds(part * rows, rows)
        for j in range(2):
            own, got = ((own_m, got_m), (own_s, got_s))[j]
            bias = (row_m, row_s)[j]
            out = dot(a, own[...]) + dot(b, got[...]) + bias[:, pl.ds(bias.shape[1] - ff, ff)]
            pre[j, at, :] = out
            hidden[j, at, :] = half(gelu(out))


def mlp_back_kernel(g_near, g_far, pre, *refs):
    g_near, g_far = Pair(g_near), Pair(g_far)
    up, down, (grad_pre, near, far, sums) = refs[:4], refs[4:8], refs[8:]
    near, far = Pair(near), Pair(far)
    rows = near.rows
    total = [None, None]
    for part in range(2):
        a, b = (g_near, g_far)[part][0], (g_near, g_far)[part][1]
        at = pl.ds(part * rows, rows)
        for j in range(2):
            grad = dot(a, down[2 * j][...]) + dot(b, down[2 * j + 1][...])
            grad = half(grad * gelu_slope(pre[j, at, :]))
            grad_pre[j, at, :] = grad
            term = row_sum(wide(grad))
            total[j] = term if part == 0 else total[j] + term
        for i in range(2):
            out = tail_dot(grad_pre[0, at, :], up[i][...]) + tail_dot(grad_pre[1, at, :], up[2 + i][...])
            if part == 0:
                near[i] = out
            else:
                far[i] = half(out)
    sums[0:1, :] = total[0]
    sums[1:2, :] = total[1]


def ff_weight_kernel(near, far, ff, keep0, keep1, send0, send1):
    near, far = Pair(near), Pair(far)
    rows = near.rows
    for j in range(2):
        for i in range(2):
            out = lead_dot(near[i], ff[j, :rows, :]) + lead_dot(far[i], ff[j, rows:, :])
            ((keep0, keep1), (send0, send1))[j][i][...] = half(out)


def down_kernel(hidden, own_m, got_m, own_s, got_s, near, far):
    near, far = Pair(near), Pair(far)
    rows = near.rows
    for part in range(2):
        at = pl.ds(part * rows, rows)
        for i in range(2):
            w_m, w_s = ((own_m, own_s), (got_m, got_s))[i]
            out = tail_dot(hidden[0, at, :], w_m[...]) + tail_dot(hidden[1, at, :], w_s[...])
            if part == 0:
                near[i] = out
            else:
                far[i] = half(out)


def layer_out_kernel(near, far, two_ref, mods, g_ref, gm_ref, out, sums):
    near, far, two_ref, g_ref, gm_ref, out = (Pair(v) for v in (near, far, two_ref, g_ref, gm_ref, out))
    for i in range(2):
        mlp_out = near[i] + wide(far[i]) + mods[i, 8:9, :]
        out[i] = half(two_ref[i] + mods[i, 5:6, :] * mlp_out)
        sums[i, 0:1, :] = row_sum(wide(g_ref[i]) * mlp_out)
        sums[i, 1:2, :] = row_sum(wide(gm_ref[i]))


def project_back_kernel(gq, keep, got, own_m, got_m, own_s, got_s, near, far, grad_m, grad_s, sums):
    near, far = Pair(near), Pair(far)
    own_m, got_m, own_s, got_s = (Pair(w, 3) for w in (own_m, got_m, own_s, got_s))
    block = own_m.rows
    rows = near.rows
    for part in range(2):
        at = pl.ds(part * rows, rows)
        total = [None, None]
        for i in range(3):
            for j in range(2):
                if i == 0:
                    g = gq[at, pl.ds(j * block, block)]
                else:
                    lanes = pl.ds(((i - 1) * 2 + j) * block, block)
                    g = half(keep[at, lanes] + wide(got[at, lanes]))
                (grad_m, grad_s)[j][at, pl.ds(i * block, block)] = g
                for n in range(2):
                    w = ((own_m, got_m), (own_s, got_s))[j][n]
                    term = dot(g, w[i])
                    total[n] = term if total[n] is None else total[n] + term
        for n in range(2):
            if part == 0:
                near[n] = total[n]
            else:
                far[n] = half(total[n])
    sums[0:1, :] = row_sum(wide(grad_m[...]))
    sums[1:2, :] = row_sum(wide(grad_s[...]))


def project_weight_kernel(near, far, grad_m, grad_s, keep0, keep1, send0, send1):
    near, far = Pair(near), Pair(far)
    rows = near.rows
    for j in range(2):
        grad = (grad_m, grad_s)[j]
        block = grad.shape[1] // 3
        for i in range(2):
            out = Pair(((keep0, keep1), (send0, send1))[j][i], 3)
            for n in range(3):
                g_near = grad[:rows, pl.ds(n * block, block)]
                g_far = grad[rows:, pl.ds(n * block, block)]
                out[n] = half(lead_dot(g_near, near[i]) + lead_dot(g_far, far[i]))


def norm_back_kernel(x_ref, mods, near, far, one_ref, out, sums):
    x_ref, near, far, one_ref, out = (Pair(v) for v in (x_ref, near, far, one_ref, out))
    normed, inv_std = layer_norm([wide(x_ref[0]), wide(x_ref[1])])
    grads = [near[i] + wide(far[i]) for i in range(2)]
    back = layer_norm_back([grads[i] * (1.0 + mods[i, 1:2, :]) for i in range(2)], normed, inv_std)
    for i in range(2):
        out[i] = half(one_ref[i] + back[i])
        sums[i, 0:1, :] = row_sum(grads[i])
        sums[i, 1:2, :] = row_sum(grads[i] * normed[i])


def dp_pairs(step):
    return [(i, i ^ step) for i in range(lax.axis_size("dp"))]


def by_halves(value):
    count = lax.axis_size("dp")
    return count & (count - 1) == 0 and value.shape[0] % count == 0


def dp_steps():
    return [1 << i for i in range(lax.axis_size("dp").bit_length() - 1)]


def reduce_sent(value, step):
    mid = value.shape[0] // 2
    upper = (lax.axis_index("dp") & step) != 0
    low, high = value[:mid], value[mid:]
    got = lax.ppermute(jnp.where(upper, low, high), "dp", dp_pairs(step))
    return jnp.where(upper, high, low), got


def reduce_got(kept, got):
    return half(wide(kept) + wide(got))


def gather_sent(value, step):
    return value, lax.ppermute(value, "dp", dp_pairs(step))


def gather_got(value, got, step):
    upper = (lax.axis_index("dp") & step) != 0
    return cat((jnp.where(upper, got, value), jnp.where(upper, value, got)), 0)


class DpSum:
    def __init__(self, value):
        self.value, self.flying = value, ()
        if by_halves(value):
            self.todo = [(True, step) for step in dp_steps()]
            self.todo += [(False, step) for step in reversed(dp_steps())]
        else:
            self.todo = []
            self.value = lax.psum(value, "dp")

    def send(self):
        if self.todo:
            reduce, step = self.todo[0]
            self.flying = (reduce_sent if reduce else gather_sent)(self.value, step)

    def land(self):
        if self.flying:
            reduce, step = self.todo.pop(0)
            if reduce:
                self.value = reduce_got(*self.flying)
            else:
                self.value = gather_got(*self.flying, step)
            self.flying = ()

    def next(self):
        self.land()
        self.send()

    def finish(self):
        self.land()
        while self.todo:
            self.send()
            self.land()
        return self.value


def tie_sums(sums, *values):
    flying = [v for one in sums for v in one.flying]
    out = tie(*values, *flying)
    rest = list(out[len(values) :])
    for one in sums:
        one.flying = tuple(rest.pop(0) for _ in one.flying)
        one.land()
    return out[: len(values)]


def small_sum_over_dp(value):
    if lax.axis_size("dp") != 4:
        return lax.psum(value, "dp")
    return value + sum(lax.ppermute(value, "dp", dp_pairs(i)) for i in range(1, 4))


def on_device(
    latents_in,
    text_emb,
    time_emb,
    shift_table,
    q_weight,
    k_weight,
    v_weight,
    q_bias,
    v_bias,
    o_weight,
    o_bias,
    cq_weight,
    cq_bias,
    ck_weight,
    cv_weight,
    cv_bias,
    co_weight,
    co_bias,
    up_weight,
    up_bias,
    down_weight,
    down_bias,
    cotangent,
):
    row = lax.axis_index("row")
    y = lax.axis_index("col")
    same = row // 2 == y
    first_col = y == 0
    part = D // 2
    text_rows = text_emb.shape[0] // 2
    block = q_weight.shape[1]
    quarter = block // 2
    ff = up_weight.shape[1]
    own = latents_in.shape[0] // 2
    tokens = 2 * own
    pair_wide, pair_half = shape((own, D), FLOAT), shape((own, D), HALF)

    def in_order(mine, other):
        return jnp.where(first_col, cat((mine, other), 0), cat((other, mine), 0))

    latents = tokens_got(*tokens_sent(latents_in, y), same)
    mods = wide(shift_table)[None] + wide(time_emb)
    row_own = cat((wide(cat((q_bias, v_bias, cq_bias, cv_bias), 0))[None], wide(up_bias)[None]), 0)
    out_bias = jnp.stack([wide(v) for v in (o_bias, co_bias, down_bias)])
    small_got = to_y(cat((jnp.where(first_col, mods[1], mods[0]), out_bias, row_own), 0))
    qkv_own, small_got = tie(cat((q_weight.T, k_weight.T, v_weight.T), 1), small_got)
    mods = jnp.stack((cat((jnp.where(first_col, mods[0], mods[1]), out_bias), 0), small_got[:9]))
    (row_m,) = call(
        bias_kernel,
        [shape((1, 4 * block + ff), FLOAT)],
        [first_col.astype(jnp.int32).reshape(1), row_own, small_got[9:]],
        smem=(0,),
    )
    row_s = to_core(row_m)
    far_rows = to_x(cat((row_m, row_s), 0))

    qkv_got = to_y(qkv_own)
    qkv_core = to_core(qkv_own)
    o_core = to_core(o_weight)
    down_own = down_weight.T
    up_core, down_core = to_core(up_weight), to_core(down_own)
    text_own = jnp.where(first_col, text_emb[:text_rows], text_emb[text_rows:])
    text_sent = jnp.where(first_col, text_emb[text_rows:], text_emb[:text_rows])
    o_own, up_own = o_weight, up_weight
    cqo_own, ckv_own = cat((cq_weight.T, co_weight), 1), cat((ck_weight.T, cv_weight.T), 1)
    latents, cqo_own, ckv_own = tie(latents, cqo_own, ckv_own)
    cqo_got = to_y(cqo_own)
    o_got = to_y(o_own)
    (h_one,) = call(norm_kernel, [pair_half], [latents, mods])
    h_one_far = to_x(h_one)

    h_one_far, qkv_got, cqo_own, ckv_own = tie(h_one_far, qkv_got, cqo_own, ckv_own)
    cqo_x = to_x(cqo_own)
    ckv_got = to_y(ckv_own)
    text_got = to_y(text_sent)
    qkv = [qkv_own, qkv_got, qkv_core, to_core(qkv_got)]
    query, kv = call(
        project_kernel,
        [shape((tokens, 2 * block), HALF), shape((tokens, 4 * block), HALF)],
        [h_one, h_one_far] + qkv + [row_m, row_s],
    )
    query, kv, cqo_got, far_rows = tie(query, kv, cqo_got, far_rows)
    cqo_got_x = to_x(cqo_got)
    kv_far = to_core(kv)
    mid = part // 2
    up_got = [to_y(up_own[:mid]), to_y(up_own[mid:])]
    attended, lse = call(
        attend_kernel,
        [shape((tokens, 2 * block), HALF), shape((2 * block // HD, tokens), FLOAT)],
        [query, kv, kv_far],
    )
    attended, o_got, cqo_x, ckv_got, text_got = tie(attended, o_got, cqo_x, ckv_got, text_got)
    (text_two,) = call(
        text_kernel, [shape((text_rows, 2 * block), HALF)], [text_own, text_got, ckv_own, ckv_got, row_m]
    )
    attended, text_two = tie(attended, text_two)
    outs = [o_own, o_got, o_core, to_core(o_got)]
    attn_near, attn_far = call(out_kernel, [pair_wide, pair_half], [attended] + outs)
    attn_far = to_x(attn_far)
    gradient = tokens_sent(cotangent, y)
    down_got = [to_y(down_own[:mid]), to_y(down_own[mid:])]

    text_near = cat((text_two, to_core(text_two)), 1)
    text_far = to_x(text_near)
    attn_far, text_far, cqo_got_x, up_got[0] = tie(attn_far, text_far, cqo_got_x, up_got[0])
    cqo_all = (
        cqo_own,
        cqo_got,
        to_core(cqo_own),
        to_core(cqo_got),
        cqo_x,
        cqo_got_x,
        to_core(cqo_x),
        to_core(cqo_got_x),
    )

    attn_out, cross_in, cross_query, cross_att, cross_lse, x_two, h_two = call(
        cross_kernel,
        [
            pair_wide,
            pair_half,
            shape((4, own, block), HALF),
            shape((4, own, block), HALF),
            shape((D // HD, own), FLOAT),
            pair_wide,
            pair_half,
        ],
        [latents, mods, attn_near, attn_far, row_m, row_s, far_rows, text_near, text_far, *cqo_all],
    )

    h_two, up_got[1] = tie(h_two, up_got[1])
    up_got = cat(up_got, 0)
    h_two_far = to_x(h_two)
    h_two_far, *gradient = tie(h_two_far, *gradient)
    gradient = tokens_got(*gradient, same)
    grad_mlp = half(cat((mods[0, 5:6], mods[1, 5:6]), 1) * wide(gradient))
    grad_mlp_far = to_x(grad_mlp)
    up = [up_own, up_got, up_core, to_core(up_got)]
    pre, hidden = call(
        up_kernel,
        [shape((2, tokens, ff), FLOAT), shape((2, tokens, ff), HALF)],
        [h_two, h_two_far] + up + [row_m, row_s],
    )
    hidden, grad_mlp_far, down_got[0] = tie(hidden, grad_mlp_far, down_got[0])

    ff_shape = shape((part, ff), HALF)
    down_keep, down_keep1, down_send, down_send1 = call(
        ff_weight_kernel, [ff_shape] * 4, [grad_mlp, grad_mlp_far, hidden]
    )
    down_keep, down_keep1, down_send, down_send1, down_got[1] = tie(
        down_keep, down_keep1, down_send, down_send1, down_got[1]
    )
    down_got = cat(down_got, 0)
    down_far = to_y(half(wide(down_keep1) + wide(to_core(down_send1))))
    down_keep = half(wide(down_keep) + wide(to_core(down_send)))
    down = [down_own, down_got, down_core, to_core(down_got)]
    grad_pre, two_near, two_far, pre_sums = call(
        mlp_back_kernel,
        [shape((2, tokens, ff), HALF), pair_wide, pair_half, shape((2, ff), FLOAT)],
        [grad_mlp, grad_mlp_far, pre] + up + down,
    )
    two_far = to_x(two_far)
    up_keep, up_keep1, up_send, up_send1 = call(
        ff_weight_kernel, [ff_shape] * 4, [h_two, h_two_far, grad_pre]
    )
    mlp_near, mlp_far = call(down_kernel, [pair_wide, pair_half], [hidden] + down)
    mlp_far, two_far, up_keep, up_keep1, up_send, up_send1 = tie(
        mlp_far, two_far, up_keep, up_keep1, up_send, up_send1
    )
    up_far = to_y(half(wide(up_keep1) + wide(to_core(up_send1))))
    up_keep = half(wide(up_keep) + wide(to_core(up_send)))

    text_shape = shape((text_rows, 4 * block), HALF)
    grad_cross, grad_cq, text_grad_near, text_grad_far, grad_x_one, grad_attn, cross_sums = call(
        cross_back_kernel,
        [
            pair_half,
            shape((4, own, block), HALF),
            text_shape,
            text_shape,
            pair_wide,
            pair_half,
            shape((2, 5, part), FLOAT),
        ],
        [gradient, mods, x_two, two_near, two_far, attn_out, cross_query, cross_lse, text_near, text_far, *cqo_all],
        [pltpu.VMEM((own, block), HALF)],
    )
    grad_attn, down_far = tie(grad_attn, down_far)
    grad_attn_far = to_x(grad_attn)
    down_sum = lax.psum(half(wide(down_keep) + wide(down_far)), "dp")
    cqo_shape = shape((block, 2 * D), HALF)
    cqo_keep, cqo_keep_x, cqo_send, cqo_send_x = call(
        cross_weight_kernel, [cqo_shape] * 4, [cross_in, grad_cross, grad_cq, cross_att]
    )
    text_grad_core = to_core(cat((text_grad_near[:, 2 * block :], text_grad_far[:, 2 * block :]), 1))
    cqo_keep = half(wide(cqo_keep) + wide(to_core(cqo_send)))
    cqo_far = half(wide(cqo_keep_x) + wide(to_core(cqo_send_x)))
    text_chip = half(
        wide(cat((text_grad_near[:, : 2 * block], text_grad_far[:, : 2 * block]), 1))
        + wide(text_grad_core)
    )
    grad_attn_far, cqo_far, text_chip = tie(grad_attn_far, cqo_far, text_chip)

    cqo_far = to_x(cqo_far)
    text_from = to_x(text_chip[:, 2 * block :])
    o_shape = shape((block, D), HALF)
    grad_att, o_keep, o_send = call(
        out_back_kernel,
        [shape((tokens, 2 * block), HALF), o_shape, o_shape],
        [grad_attn, grad_attn_far, attended] + outs,
    )
    mlp_far = to_x(mlp_far)
    grad_query, kv_keep, kv_send = call(
        attend_back_kernel,
        [
            shape((tokens, 2 * block), HALF),
            shape((tokens, 4 * block), FLOAT),
            shape((tokens, 4 * block), HALF),
        ],
        [query, kv, kv_far, lse, grad_att],
    )
    grad_query, kv_keep, kv_send, mlp_far, cqo_far, text_from, up_far, down_sum = tie(
        grad_query, kv_keep, kv_send, mlp_far, cqo_far, text_from, up_far, down_sum
    )
    up_sum = lax.psum(half(wide(up_keep) + wide(up_far)), "dp")
    kv_got = to_core(kv_send)
    rest_shape = shape((block, 5 * part), HALF)
    rest_keep, rest_far, grad_text, text_part, cv_sum = call(
        rest_kernel,
        [
            rest_shape,
            rest_shape,
            shape((text_rows, 2 * block), HALF),
            shape((text_rows, D), HALF),
            shape((1, block), FLOAT),
        ],
        [
            cqo_keep,
            cqo_far,
            text_chip[:, : 2 * block],
            text_from,
            text_own,
            text_got,
            ckv_own,
            ckv_got,
            o_keep,
            to_core(o_send),
        ],
    )
    rest_far = to_y(rest_far)
    layer_pair, layer_sums = call(
        layer_out_kernel,
        [pair_half, shape((2, 2, part), FLOAT)],
        [mlp_near, mlp_far, x_two, mods, gradient, grad_mlp],
    )
    layer_pair = halves_sent(layer_pair, same)
    text_near = to_core(text_part)
    grad_shape = shape((tokens, 3 * block), HALF)
    near, far, grad_m, grad_s, qkv_sums = call(
        project_back_kernel,
        [pair_wide, pair_half, grad_shape, grad_shape, shape((2, 3 * block), FLOAT)],
        [grad_query, kv_keep, kv_got] + qkv,
    )
    far, text_near = tie(far, text_near)
    far = to_x(far)
    text_sum = wide(text_part) + wide(text_near)
    text_got = to_x(half(text_sum))
    qkv_shape = shape((block, 3 * part), HALF)
    qkv_keep, qkv_keep1, qkv_send, qkv_send1 = call(
        project_weight_kernel, [qkv_shape] * 4, [h_one, h_one_far, grad_m, grad_s]
    )
    qkv_send, qkv_send1, qkv_keep, qkv_keep1, text_got, far, rest_far = tie(
        qkv_send, qkv_send1, qkv_keep, qkv_keep1, text_got, far, rest_far
    )
    rest_sum = DpSum(half(wide(rest_keep) + wide(rest_far)))
    rest_sum.send()
    qkv_far = to_y(half(wide(qkv_keep1) + wide(to_core(qkv_send1))))
    qkv_keep = half(wide(qkv_keep) + wide(to_core(qkv_send)))
    text_sum = text_sum + wide(text_got)
    text_far = to_y(half(text_sum[:, part:]))
    token_pair, one_sums = call(
        norm_back_kernel,
        [pair_half, shape((2, 2, part), FLOAT)],
        [latents, mods, near, far, grad_x_one],
    )
    token_pair, one_sums, qkv_far = tie_sums([rest_sum], token_pair, one_sums, qkv_far)
    qkv_sum = DpSum(half(wide(qkv_keep) + wide(qkv_far)))
    qkv_sum.send()
    rest_sum.send()
    token_sent = halves_sent(token_pair, same)

    feature_sums = cat((one_sums, cross_sums, layer_sums), 1)
    flat = feature_sums.reshape(9 * D)
    gcq_sum = jnp.sum(wide(grad_cq), 1)
    cv_sum = cv_sum[0]
    core_got = to_core(
        cat((flat, gcq_sum[3], gcq_sum[1], qkv_sums[1, :block], qkv_sums[1, 2 * block :], pre_sums[1]), 0)
    )
    core_got, text_far, up_sum = tie_sums([qkv_sum, rest_sum], core_got, text_far, up_sum)
    qkv_sum.send()
    rest_sum.send()
    text_grad = in_order(text_sum[:, :part], wide(text_far))
    chip = core_got + cat(
        (flat, gcq_sum[2], gcq_sum[0], qkv_sums[0, :block], qkv_sums[0, 2 * block :], pre_sums[0]), 0
    )
    x_got = to_x(chip[: 9 * D + block])
    (x_got,) = tie_sums([qkv_sum, rest_sum], x_got)
    qkv_sum.send()
    rest_sum.send()
    sums = (chip[: 9 * D] + x_got[: 9 * D]).reshape(2, 9, part)
    cq_row = chip[9 * D + block : 9 * D + 2 * block] + x_got[9 * D :]
    rest = chip[9 * D + 2 * block :]
    row_rows = [
        (v[: v.shape[0] // 2], v[v.shape[0] // 2 :])
        for v in (rest[:block], rest[block : 2 * block], cq_row, cv_sum, rest[2 * block :])
    ]
    row_low = cat([v[0] for v in row_rows], 0)
    row_high = cat([v[1] for v in row_rows], 0)
    row_mine = jnp.where(first_col, row_low, row_high)
    row_sent = jnp.where(first_col, row_high, row_low)
    col_got = to_y(cat((sums[1].reshape(9 * part), row_sent), 0))
    col_got, *both = tie_sums([qkv_sum, rest_sum], col_got, *token_sent, *layer_pair)
    qkv_sum.send()
    rest_sum.send()
    token_input_gradient = wide(halves_got(*both[:2], y))
    layer_out = halves_got(*both[2:], y)
    sums_got = col_got[: 9 * part].reshape(9, part)
    sums_own = sums[0]

    def six(v):
        return jnp.stack((v[0], v[1], v[5], v[2], v[3], v[7]))

    time_own, time_got = six(sums_own), six(sums_got)
    time_grad = jnp.where(first_col, jnp.stack((time_own, time_got)), jnp.stack((time_got, time_own)))
    totals = small_sum_over_dp(
        cat(((sums_own + sums_got).reshape(9 * part), row_mine + col_got[9 * part :]), 0)
    )
    table_grad = six(totals[: 9 * part].reshape(9, part))
    o_bias_grad, co_bias_grad, down_bias_grad = (
        totals[i * part : (i + 1) * part] for i in (6, 4, 8)
    )
    rows = totals[9 * part :]
    q_bias_grad, v_bias_grad, cq_bias_grad, cv_bias_grad = (
        rows[i * quarter : (i + 1) * quarter] for i in range(4)
    )
    up_bias_grad = rows[4 * quarter :]

    qkv_grad, rest_sum = qkv_sum.finish(), rest_sum.finish()
    q_grad, k_grad, v_grad = (wide(qkv_grad[:, i * part : (i + 1) * part]).T for i in range(3))
    cq_grad, co_grad, ck_grad, cv_grad, o_grad = (
        wide(rest_sum[:, i * part : (i + 1) * part]) for i in range(5)
    )
    return (
        layer_out,
        token_input_gradient,
        text_grad,
        time_grad,
        table_grad,
        q_grad,
        k_grad,
        v_grad,
        q_bias_grad,
        v_bias_grad,
        o_grad,
        o_bias_grad,
        cq_grad.T,
        cq_bias_grad,
        ck_grad.T,
        cv_grad.T,
        cv_bias_grad,
        co_grad,
        co_bias_grad,
        wide(up_sum),
        up_bias_grad,
        wide(down_sum).T,
        down_bias_grad,
    )


def solution(mesh):
    in_specs = (
        P(("dp", "row"), "col"),
        P("dp", "col"),
        P("dp", None, "col"),
        P(None, "col"),
        P("col", "row"),
        P("col", "row"),
        P("col", "row"),
        P(("row", "col")),
        P(("row", "col")),
        P("row", "col"),
        P("col"),
        P("col", "row"),
        P(("row", "col")),
        P("col", "row"),
        P("col", "row"),
        P(("row", "col")),
        P("row", "col"),
        P("col"),
        P("col", "row"),
        P(("row", "col")),
        P("row", "col"),
        P("col"),
        P(("dp", "row"), "col"),
    )
    out_specs = (
        P(("dp", "row"), "col"),
        P(("dp", "row"), "col"),
        P("dp", "col"),
        P("dp", None, "col"),
        P(None, "col"),
        P("col", "row"),
        P("col", "row"),
        P("col", "row"),
        P(("row", "col")),
        P(("row", "col")),
        P("row", "col"),
        P("col"),
        P("col", "row"),
        P(("row", "col")),
        P("col", "row"),
        P("col", "row"),
        P(("row", "col")),
        P("row", "col"),
        P("col"),
        P("col", "row"),
        P(("row", "col")),
        P("row", "col"),
        P("col"),
    )
    return jax.shard_map(
        on_device, mesh=mesh, in_specs=in_specs, out_specs=out_specs, check_vma=False
    )
```

```python
import jax
import jax.numpy as jnp
from jax import lax
from jax.experimental import pallas as pl
from jax.experimental.pallas import tpu as pltpu
from jax.sharding import PartitionSpec as P


D = 1152
HD = 72
FLOAT = jnp.float32
HALF = jnp.bfloat16
EPSILON = 1e-06
SCALE = HD ** (-0.5)
VMEM_BYTES = 48 * 1024 * 1024

CORE = [(i, i ^ 1) for i in range(4)]
ACROSS = [(i, i ^ 2) for i in range(4)]
SWAP = [(0, 1), (1, 0)]


def place(x, k, y):
    return (x * 2 + k) * 2 + y


POINTS = [(x, k, y) for x in range(2) for k in range(2) for y in range(2)]
TURN = [(place(x, k, y), place(y, k, x)) for x, k, y in POINTS]
TURN_IN = [(place(x, k, y), place(1 - y, k, x)) for x, k, y in POINTS]
TURN_OUT = [(place(x, k, y), place(y, k, 1 - x)) for x, k, y in POINTS]


def to_core(value):
    return lax.ppermute(value, "row", CORE)


def to_x(value):
    return lax.ppermute(value, "row", ACROSS)


def to_y(value):
    return lax.ppermute(value, "col", SWAP)


def tie(*values):
    return lax.optimization_barrier(values)


def dot(left, right):
    return jnp.dot(left, right, preferred_element_type=FLOAT)


def lead_dot(left, right):
    return lax.dot_general(left, right, (((0,), (0,)), ((), ())), preferred_element_type=FLOAT)


def tail_dot(left, right):
    return lax.dot_general(left, right, (((1,), (1,)), ((), ())), preferred_element_type=FLOAT)


def cat(parts, axis):
    return jnp.concatenate(parts, axis)


def half(value):
    return value.astype(HALF)


def wide(value):
    return value.astype(FLOAT)


def tokens_sent(value, y):
    mid = value.shape[0] // 2
    low, high = value[:mid], value[mid:]
    first = lax.ppermute(jnp.where(y == 0, low, high), ("row", "col"), TURN)
    return first, lax.ppermute(jnp.where(y == 0, high, low), ("row", "col"), TURN_IN)


def tokens_got(first, second, same):
    return cat((jnp.where(same, first, second), jnp.where(same, second, first)), 1)


def halves_sent(pair, same):
    mid = pair.shape[1] // 2
    low, high = pair[:, :mid], pair[:, mid:]
    first = lax.ppermute(jnp.where(same, low, high), ("row", "col"), TURN)
    return first, lax.ppermute(jnp.where(same, high, low), ("row", "col"), TURN_OUT)


def halves_got(first, second, y):
    return cat((jnp.where(y == 0, first, second), jnp.where(y == 0, second, first)), 0)


def pair_mean(pair):
    return (jnp.sum(pair[0], 1, keepdims=True) + jnp.sum(pair[1], 1, keepdims=True)) / D


def layer_norm(pair):
    average = pair_mean(pair)
    center = [v - average for v in pair]
    inv_std = lax.rsqrt(pair_mean([c * c for c in center]) + EPSILON)
    return [c * inv_std for c in center], inv_std


def layer_norm_back(grad, normed, inv_std):
    average = pair_mean(grad)
    crossed = pair_mean([g * n for g, n in zip(grad, normed)])
    return [inv_std * (g - average - n * crossed) for g, n in zip(grad, normed)]


def row_sum(value):
    return jnp.sum(value, 0, keepdims=True)


def gelu(v):
    return 0.5 * v * (1.0 + jnp.tanh(0.7978845608028654 * (v + 0.044715 * v * v * v)))


def gelu_slope(v):
    t = jnp.tanh(0.7978845608028654 * (v + 0.044715 * v * v * v))
    return 0.5 * (1.0 + t) + 0.5 * v * (1.0 - t * t) * 0.7978845608028654 * (
        1.0 + 3.0 * 0.044715 * v * v
    )


def call(kernel, outs, args, scratch=(), smem=()):
    vmem = pl.BlockSpec(memory_space=pltpu.VMEM)
    specs = [pl.BlockSpec(memory_space=pltpu.SMEM) if i in smem else vmem for i in range(len(args))]
    return pl.pallas_call(
        kernel,
        out_shape=outs,
        in_specs=specs,
        out_specs=[vmem] * len(outs),
        scratch_shapes=scratch,
        compiler_params=pltpu.CompilerParams(vmem_limit_bytes=VMEM_BYTES),
        cost_estimate=pl.CostEstimate(flops=1, bytes_accessed=1, transcendentals=0),
    )(*args)


class Pair:
    def __init__(self, ref, count=2):
        self.ref, self.size, self.rows = ref, ref.shape[1] // count, ref.shape[0]

    def __getitem__(self, i):
        return self.ref[:, pl.ds(i * self.size, self.size)]

    def __setitem__(self, i, value):
        self.ref[:, pl.ds(i * self.size, self.size)] = value


def shape(dims, dtype):
    return jax.ShapeDtypeStruct(dims, dtype)


def bias_kernel(first_col, own, got, out):
    quarter = own.shape[1] // 4
    low_own = first_col[0] == 1
    at = 0
    for r, begin, size in [(0, i * quarter, quarter) for i in range(4)] + [(1, 0, 4 * quarter)]:
        a, b = own[r : r + 1, pl.ds(begin, size)], got[r : r + 1, pl.ds(begin, size)]
        out[:, pl.ds(at, size)] = jnp.where(low_own, a, b)
        out[:, pl.ds(at + size, size)] = jnp.where(low_own, b, a)
        at += 2 * size


def norm_kernel(x_ref, mods, out):
    x_ref, out = Pair(x_ref), Pair(out)
    normed, _ = layer_norm([wide(x_ref[0]), wide(x_ref[1])])
    for i in range(2):
        out[i] = half(normed[i] * (1.0 + mods[i, 1:2, :]) + mods[i, 0:1, :])


def project_kernel(near, far, own_m, got_m, own_s, got_s, row_m, row_s, q_out, kv_out):
    near, far = Pair(near), Pair(far)
    own_m, got_m, own_s, got_s = (Pair(w, 3) for w in (own_m, got_m, own_s, got_s))
    block = own_m.rows
    rows = near.rows
    for part in range(2):
        a, b = (near, far)[part][0], (near, far)[part][1]
        at = pl.ds(part * rows, rows)
        for i in range(3):
            for j in range(2):
                own, got = ((own_m, got_m), (own_s, got_s))[j]
                bias = (row_m, row_s)[j]
                out = tail_dot(a, own[i]) + tail_dot(b, got[i])
                if i == 0:
                    q_out[at, pl.ds(j * block, block)] = half(out + bias[:, :block])
                else:
                    if i == 2:
                        out = out + bias[:, block : 2 * block]
                    kv_out[at, pl.ds(((i - 1) * 2 + j) * block, block)] = half(out)


def attend_head(q, k, v):
    scores = tail_dot(k, q) * SCALE
    peak = jnp.max(scores, 0, keepdims=True)
    raised = jnp.exp(scores - peak)
    summed = jnp.sum(raised, 0, keepdims=True)
    mixed = dot(v.T, half(raised)) / summed
    return half(mixed.T), peak + jnp.log(summed)


def attend_head_back(q, k, v, g, lse):
    prob = jnp.exp(tail_dot(k, q) * SCALE - lse)
    grad_prob = tail_dot(v, g)
    centre = jnp.sum(prob * grad_prob, 0, keepdims=True)
    grad_score = half(prob * (grad_prob - centre))
    grad_q = (dot(k.T, grad_score) * SCALE).T
    grad_k = dot(grad_score, q) * SCALE
    grad_v = dot(half(prob), g)
    return grad_q, grad_k, grad_v


def attend_kernel(q_ref, near, far, out_ref, lse_ref):
    heads = q_ref.shape[1] // HD
    width = heads * HD
    for h in range(heads):
        at = pl.ds(h * HD, HD)
        there = (h + heads // 2) % heads * HD
        k = cat((near[:, at], far[:, pl.ds(there, HD)]), 0)
        v = cat((near[:, pl.ds(width + h * HD, HD)], far[:, pl.ds(width + there, HD)]), 0)
        for c in range(2):
            rows = pl.ds(c * (q_ref.shape[0] // 2), q_ref.shape[0] // 2)
            mixed, lse = attend_head(q_ref[rows, at], k, v)
            out_ref[rows, at] = mixed
            lse_ref[pl.ds(h, 1), rows] = lse


def attend_back_kernel(q_ref, near, far, lse_ref, g_ref, gq_ref, keep_ref, send_ref):
    heads = q_ref.shape[1] // HD
    width = heads * HD
    tokens = near.shape[0]
    for h in range(heads):
        at = pl.ds(h * HD, HD)
        there = (h + heads // 2) % heads * HD
        k = cat((near[:, at], far[:, pl.ds(there, HD)]), 0)
        v = cat((near[:, pl.ds(width + h * HD, HD)], far[:, pl.ds(width + there, HD)]), 0)
        total_k, total_v = None, None
        for c in range(2):
            rows = pl.ds(c * (q_ref.shape[0] // 2), q_ref.shape[0] // 2)
            gq, gk, gv = attend_head_back(
                q_ref[rows, at], k, v, g_ref[rows, at], lse_ref[pl.ds(h, 1), rows]
            )
            gq_ref[rows, at] = half(gq)
            total_k = gk if total_k is None else total_k + gk
            total_v = gv if total_v is None else total_v + gv
        keep_ref[:, at] = total_k[:tokens]
        keep_ref[:, pl.ds(width + h * HD, HD)] = total_v[:tokens]
        send_ref[:, pl.ds(there, HD)] = half(total_k[tokens:])
        send_ref[:, pl.ds(width + there, HD)] = half(total_v[tokens:])


def out_kernel(att, own_m, got_m, own_s, got_s, near, far):
    near, far = Pair(near), Pair(far)
    block = own_m.shape[0]
    rows = near.rows
    for part in range(2):
        at = pl.ds(part * rows, rows)
        a, b = att[at, :block], att[at, pl.ds(block, block)]
        for i in range(2):
            w_m, w_s = ((own_m, own_s), (got_m, got_s))[i]
            out = dot(a, w_m[...]) + dot(b, w_s[...])
            if part == 0:
                near[i] = out
            else:
                far[i] = half(out)


def out_back_kernel(near, far, att, own_m, got_m, own_s, got_s, grad_att, keep, send):
    near, far, keep, send = Pair(near), Pair(far), Pair(keep), Pair(send)
    block = own_m.shape[0]
    rows = near.rows
    for part in range(2):
        at = pl.ds(part * rows, rows)
        a, b = (near, far)[part][0], (near, far)[part][1]
        for j in range(2):
            own, got = ((own_m, got_m), (own_s, got_s))[j]
            grad_att[at, pl.ds(j * block, block)] = half(tail_dot(a, own[...]) + tail_dot(b, got[...]))
    for j in range(2):
        a = att[:rows, pl.ds(j * block, block)]
        b = att[rows:, pl.ds(j * block, block)]
        for i in range(2):
            (keep, send)[j][i] = half(lead_dot(a, near[i]) + lead_dot(b, far[i]))


def text_kernel(near, other, own, got, row_m, out):
    own, got = Pair(own), Pair(got)
    block = own.rows
    for i in range(2):
        sums = tail_dot(near[...], own[i]) + tail_dot(other[...], got[i])
        if i == 1:
            sums = sums + row_m[:, pl.ds(3 * block, block)]
        out[:, pl.ds(i * block, block)] = half(sums)


def cross_kernel(x_ref, mods, near, far, row_m, row_s, far_rows, text_near, text_far, *refs):
    weights = [Pair(w) for w in refs[:8]]
    x_ref, near, far = Pair(x_ref), Pair(near), Pair(far)
    attn_out, cross_in, q_out, att_out, lse_ref, two_ref, h_ref = refs[8:]
    attn_out, cross_in, two_ref, h_ref = (Pair(v) for v in (attn_out, cross_in, two_ref, h_ref))
    block = weights[0].rows
    for i in range(2):
        attn = near[i] + wide(far[i]) + mods[i, 6:7, :]
        attn_out[i] = attn
        one = wide(x_ref[i]) + mods[i, 2:3, :] * attn
        cross_in[i] = half(one)
        two_ref[i] = one + mods[i, 7:8, :]
    a, b = cross_in[0], cross_in[1]
    for n in range(4):
        pair = weights[2 * n], weights[2 * n + 1]
        bias = (row_m[...], row_s[...], far_rows[0:1, :], far_rows[1:2, :])[n]
        bias = bias[:, 2 * block : 3 * block]
        q_out[n] = half(tail_dot(a, pair[0][0]) + tail_dot(b, pair[1][0]) + bias)
        text = (text_near, text_far)[n // 2]
        base = (n % 2) * 2 * block
        for h in range(block // HD):
            at = pl.ds(h * HD, HD)
            mixed, lse = attend_head(
                q_out[n, :, at],
                text[:, pl.ds(base + h * HD, HD)],
                text[:, pl.ds(base + block + h * HD, HD)],
            )
            att_out[n, :, at] = mixed
            lse_ref[pl.ds(n * (block // HD) + h, 1), :] = lse
        att = att_out[n]
        for i in range(2):
            two_ref[i] += dot(att, pair[i][1])
    normed, _ = layer_norm([two_ref[0], two_ref[1]])
    for i in range(2):
        h_ref[i] = half(normed[i] * (1.0 + mods[i, 4:5, :]) + mods[i, 3:4, :])


def cross_back_kernel(g_ref, mods, two_ref, near, far, attn_out, q_ref, lse_ref, text_near, text_far, *refs):
    weights = [Pair(w) for w in refs[:8]]
    g_ref, two_ref, near, far, attn_out = (Pair(v) for v in (g_ref, two_ref, near, far, attn_out))
    grad_cross, gq_out, near_out, far_out, one_ref, grad_attn, sums, grad_scratch = refs[8:]
    grad_cross, one_ref, grad_attn = Pair(grad_cross), Pair(one_ref), Pair(grad_attn)
    block = weights[0].rows
    normed, inv_std = layer_norm([two_ref[0], two_ref[1]])
    grads = [near[i] + wide(far[i]) for i in range(2)]
    back = layer_norm_back([grads[i] * (1.0 + mods[i, 4:5, :]) for i in range(2)], normed, inv_std)
    for i in range(2):
        sums[i, 0:1, :] = row_sum(grads[i])
        sums[i, 1:2, :] = row_sum(grads[i] * normed[i])
        grad = wide(g_ref[i]) + back[i]
        one_ref[i] = grad
        grad_cross[i] = half(grad)
        sums[i, 2:3, :] = row_sum(wide(half(grad)))
    a, b = grad_cross[0], grad_cross[1]
    for n in range(4):
        pair = weights[2 * n], weights[2 * n + 1]
        grad_scratch[...] = half(tail_dot(a, pair[0][1]) + tail_dot(b, pair[1][1]))
        text, text_out = ((text_near, near_out), (text_far, far_out))[n // 2]
        base = (n % 2) * 2 * block
        for h in range(block // HD):
            at = pl.ds(h * HD, HD)
            k_at, v_at = pl.ds(base + h * HD, HD), pl.ds(base + block + h * HD, HD)
            gq, gk, gv = attend_head_back(
                q_ref[n, :, at],
                text[:, k_at],
                text[:, v_at],
                grad_scratch[:, at],
                lse_ref[pl.ds(n * (block // HD) + h, 1), :],
            )
            gq_out[n, :, at] = half(gq)
            text_out[:, k_at] = half(gk)
            text_out[:, v_at] = half(gv)
        gq = gq_out[n]
        for i in range(2):
            one_ref[i] += dot(gq, pair[i][0])
    for i in range(2):
        one = one_ref[i]
        attn = half(one * mods[i, 2:3, :])
        grad_attn[i] = attn
        sums[i, 3:4, :] = row_sum(one * attn_out[i])
        sums[i, 4:5, :] = row_sum(wide(attn))


def cross_weight_kernel(x_ref, g_ref, q_ref, att_ref, keep_m, keep_x, send_m, send_x):
    x_ref, g_ref = Pair(x_ref), Pair(g_ref)
    for n, out in enumerate((keep_m, send_m, keep_x, send_x)):
        out = Pair(out, 4)
        for i in range(2):
            out[2 * i] = half(lead_dot(q_ref[n], x_ref[i]))
            out[2 * i + 1] = half(lead_dot(att_ref[n], g_ref[i]))


def rest_kernel(cqo, cqo_got, text_near, text_got, text_own, text_other, ckv_own, ckv_got, o_ref, o_got, *refs):
    outs, (grad_text, text_part, cv_sum) = refs[:2], refs[2:]
    cqo, cqo_got, o_ref, o_got, text_part = (
        Pair(cqo, 4), Pair(cqo_got, 4), Pair(o_ref), Pair(o_got), Pair(text_part)
    )
    grad_text[...] = half(wide(text_near[...]) + wide(text_got[...]))
    block = cqo.rows
    gk, gv = grad_text[:, :block], grad_text[:, pl.ds(block, block)]
    cv_sum[...] = row_sum(wide(gv))
    for i in range(2):
        out, text, weight = Pair(outs[i], 5), (text_own, text_other)[i], Pair((ckv_own, ckv_got)[i])
        for n in range(2):
            out[n] = half(wide(cqo[2 * i + n]) + wide(cqo_got[2 * i + n]))
        out[2] = half(lead_dot(gk, text[...]))
        out[3] = half(lead_dot(gv, text[...]))
        out[4] = half(wide(o_ref[i]) + wide(o_got[i]))
        text_part[i] = half(dot(gk, weight[0]) + dot(gv, weight[1]))


def up_kernel(near, far, own_m, got_m, own_s, got_s, row_m, row_s, pre, hidden):
    near, far = Pair(near), Pair(far)
    rows, ff = near.rows, own_m.shape[1]
    for part in range(2):
        a, b = (near, far)[part][0], (near, far)[part][1]
        at = pl.ds(part * rows, rows)
        for j in range(2):
            own, got = ((own_m, got_m), (own_s, got_s))[j]
            bias = (row_m, row_s)[j]
            out = dot(a, own[...]) + dot(b, got[...]) + bias[:, pl.ds(bias.shape[1] - ff, ff)]
            pre[j, at, :] = out
            hidden[j, at, :] = half(gelu(out))


def mlp_back_kernel(g_near, g_far, pre, *refs):
    g_near, g_far = Pair(g_near), Pair(g_far)
    up, down, (grad_pre, near, far, sums) = refs[:4], refs[4:8], refs[8:]
    near, far = Pair(near), Pair(far)
    rows = near.rows
    total = [None, None]
    for part in range(2):
        a, b = (g_near, g_far)[part][0], (g_near, g_far)[part][1]
        at = pl.ds(part * rows, rows)
        for j in range(2):
            grad = dot(a, down[2 * j][...]) + dot(b, down[2 * j + 1][...])
            grad = half(grad * gelu_slope(pre[j, at, :]))
            grad_pre[j, at, :] = grad
            term = row_sum(wide(grad))
            total[j] = term if part == 0 else total[j] + term
        for i in range(2):
            out = tail_dot(grad_pre[0, at, :], up[i][...]) + tail_dot(grad_pre[1, at, :], up[2 + i][...])
            if part == 0:
                near[i] = out
            else:
                far[i] = half(out)
    sums[0:1, :] = total[0]
    sums[1:2, :] = total[1]


def ff_weight_kernel(near, far, ff, keep0, keep1, send0, send1):
    near, far = Pair(near), Pair(far)
    rows = near.rows
    for j in range(2):
        for i in range(2):
            out = lead_dot(near[i], ff[j, :rows, :]) + lead_dot(far[i], ff[j, rows:, :])
            ((keep0, keep1), (send0, send1))[j][i][...] = half(out)


def down_kernel(hidden, own_m, got_m, own_s, got_s, near, far):
    near, far = Pair(near), Pair(far)
    rows = near.rows
    for part in range(2):
        at = pl.ds(part * rows, rows)
        for i in range(2):
            w_m, w_s = ((own_m, own_s), (got_m, got_s))[i]
            out = tail_dot(hidden[0, at, :], w_m[...]) + tail_dot(hidden[1, at, :], w_s[...])
            if part == 0:
                near[i] = out
            else:
                far[i] = half(out)


def layer_out_kernel(near, far, two_ref, mods, g_ref, gm_ref, out, sums):
    near, far, two_ref, g_ref, gm_ref, out = (Pair(v) for v in (near, far, two_ref, g_ref, gm_ref, out))
    for i in range(2):
        mlp_out = near[i] + wide(far[i]) + mods[i, 8:9, :]
        out[i] = half(two_ref[i] + mods[i, 5:6, :] * mlp_out)
        sums[i, 0:1, :] = row_sum(wide(g_ref[i]) * mlp_out)
        sums[i, 1:2, :] = row_sum(wide(gm_ref[i]))


def project_back_kernel(gq, keep, got, own_m, got_m, own_s, got_s, near, far, grad_m, grad_s, sums):
    near, far = Pair(near), Pair(far)
    own_m, got_m, own_s, got_s = (Pair(w, 3) for w in (own_m, got_m, own_s, got_s))
    block = own_m.rows
    rows = near.rows
    for part in range(2):
        at = pl.ds(part * rows, rows)
        total = [None, None]
        for i in range(3):
            for j in range(2):
                if i == 0:
                    g = gq[at, pl.ds(j * block, block)]
                else:
                    lanes = pl.ds(((i - 1) * 2 + j) * block, block)
                    g = half(keep[at, lanes] + wide(got[at, lanes]))
                (grad_m, grad_s)[j][at, pl.ds(i * block, block)] = g
                for n in range(2):
                    w = ((own_m, got_m), (own_s, got_s))[j][n]
                    term = dot(g, w[i])
                    total[n] = term if total[n] is None else total[n] + term
        for n in range(2):
            if part == 0:
                near[n] = total[n]
            else:
                far[n] = half(total[n])
    sums[0:1, :] = row_sum(wide(grad_m[...]))
    sums[1:2, :] = row_sum(wide(grad_s[...]))


def project_weight_kernel(near, far, grad_m, grad_s, keep0, keep1, send0, send1):
    near, far = Pair(near), Pair(far)
    rows = near.rows
    for j in range(2):
        grad = (grad_m, grad_s)[j]
        block = grad.shape[1] // 3
        for i in range(2):
            out = Pair(((keep0, keep1), (send0, send1))[j][i], 3)
            for n in range(3):
                g_near = grad[:rows, pl.ds(n * block, block)]
                g_far = grad[rows:, pl.ds(n * block, block)]
                out[n] = half(lead_dot(g_near, near[i]) + lead_dot(g_far, far[i]))


def norm_back_kernel(x_ref, mods, near, far, one_ref, out, sums):
    x_ref, near, far, one_ref, out = (Pair(v) for v in (x_ref, near, far, one_ref, out))
    normed, inv_std = layer_norm([wide(x_ref[0]), wide(x_ref[1])])
    grads = [near[i] + wide(far[i]) for i in range(2)]
    back = layer_norm_back([grads[i] * (1.0 + mods[i, 1:2, :]) for i in range(2)], normed, inv_std)
    for i in range(2):
        out[i] = half(one_ref[i] + back[i])
        sums[i, 0:1, :] = row_sum(grads[i])
        sums[i, 1:2, :] = row_sum(grads[i] * normed[i])


def dp_pairs(step):
    return [(i, i ^ step) for i in range(lax.axis_size("dp"))]


def by_halves(value):
    count = lax.axis_size("dp")
    return count & (count - 1) == 0 and value.shape[0] % count == 0


def dp_steps():
    return [1 << i for i in range(lax.axis_size("dp").bit_length() - 1)]


def reduce_sent(value, step):
    mid = value.shape[0] // 2
    upper = (lax.axis_index("dp") & step) != 0
    low, high = value[:mid], value[mid:]
    got = lax.ppermute(jnp.where(upper, low, high), "dp", dp_pairs(step))
    return jnp.where(upper, high, low), got


def reduce_got(kept, got):
    return half(wide(kept) + wide(got))


def gather_sent(value, step):
    return value, lax.ppermute(value, "dp", dp_pairs(step))


def gather_got(value, got, step):
    upper = (lax.axis_index("dp") & step) != 0
    return cat((jnp.where(upper, got, value), jnp.where(upper, value, got)), 0)


class DpSum:
    def __init__(self, value):
        self.value, self.flying = value, ()
        if by_halves(value):
            self.todo = [(True, step) for step in dp_steps()]
            self.todo += [(False, step) for step in reversed(dp_steps())]
        else:
            self.todo = []
            self.value = lax.psum(value, "dp")

    def send(self):
        if self.todo:
            reduce, step = self.todo[0]
            self.flying = (reduce_sent if reduce else gather_sent)(self.value, step)

    def land(self):
        if self.flying:
            reduce, step = self.todo.pop(0)
            if reduce:
                self.value = reduce_got(*self.flying)
            else:
                self.value = gather_got(*self.flying, step)
            self.flying = ()

    def next(self):
        self.land()
        self.send()

    def finish(self):
        self.land()
        while self.todo:
            self.send()
            self.land()
        return self.value


def tie_sums(sums, *values):
    flying = [v for one in sums for v in one.flying]
    out = tie(*values, *flying)
    rest = list(out[len(values) :])
    for one in sums:
        one.flying = tuple(rest.pop(0) for _ in one.flying)
        one.land()
    return out[: len(values)]


def small_sum_over_dp(value):
    if lax.axis_size("dp") != 4:
        return lax.psum(value, "dp")
    return value + sum(lax.ppermute(value, "dp", dp_pairs(i)) for i in range(1, 4))


def on_device(
    latents_in,
    text_emb,
    time_emb,
    shift_table,
    q_weight,
    k_weight,
    v_weight,
    q_bias,
    v_bias,
    o_weight,
    o_bias,
    cq_weight,
    cq_bias,
    ck_weight,
    cv_weight,
    cv_bias,
    co_weight,
    co_bias,
    up_weight,
    up_bias,
    down_weight,
    down_bias,
    cotangent,
):
    row = lax.axis_index("row")
    y = lax.axis_index("col")
    same = row // 2 == y
    first_col = y == 0
    part = D // 2
    text_rows = text_emb.shape[0] // 2
    block = q_weight.shape[1]
    quarter = block // 2
    ff = up_weight.shape[1]
    own = latents_in.shape[0] // 2
    tokens = 2 * own
    pair_wide, pair_half = shape((own, D), FLOAT), shape((own, D), HALF)

    def in_order(mine, other):
        return jnp.where(first_col, cat((mine, other), 0), cat((other, mine), 0))

    latents = tokens_got(*tokens_sent(latents_in, y), same)
    mods = wide(shift_table)[None] + wide(time_emb)
    row_own = cat((wide(cat((q_bias, v_bias, cq_bias, cv_bias), 0))[None], wide(up_bias)[None]), 0)
    out_bias = jnp.stack([wide(v) for v in (o_bias, co_bias, down_bias)])
    small_got = to_y(cat((jnp.where(first_col, mods[1], mods[0]), out_bias, row_own), 0))
    qkv_own, small_got = tie(cat((q_weight.T, k_weight.T, v_weight.T), 1), small_got)
    mods = jnp.stack((cat((jnp.where(first_col, mods[0], mods[1]), out_bias), 0), small_got[:9]))
    (row_m,) = call(
        bias_kernel,
        [shape((1, 4 * block + ff), FLOAT)],
        [first_col.astype(jnp.int32).reshape(1), row_own, small_got[9:]],
        smem=(0,),
    )
    row_s = to_core(row_m)
    far_rows = to_x(cat((row_m, row_s), 0))

    qkv_got = to_y(qkv_own)
    qkv_core = to_core(qkv_own)
    o_core = to_core(o_weight)
    down_own = down_weight.T
    up_core, down_core = to_core(up_weight), to_core(down_own)
    text_own = jnp.where(first_col, text_emb[:text_rows], text_emb[text_rows:])
    text_sent = jnp.where(first_col, text_emb[text_rows:], text_emb[:text_rows])
    o_own, up_own = o_weight, up_weight
    cqo_own, ckv_own = cat((cq_weight.T, co_weight), 1), cat((ck_weight.T, cv_weight.T), 1)
    latents, cqo_own, ckv_own = tie(latents, cqo_own, ckv_own)
    cqo_got = to_y(cqo_own)
    o_got = to_y(o_own)
    (h_one,) = call(norm_kernel, [pair_half], [latents, mods])
    h_one_far = to_x(h_one)

    h_one_far, qkv_got, cqo_own, ckv_own = tie(h_one_far, qkv_got, cqo_own, ckv_own)
    cqo_x = to_x(cqo_own)
    ckv_got = to_y(ckv_own)
    text_got = to_y(text_sent)
    qkv = [qkv_own, qkv_got, qkv_core, to_core(qkv_got)]
    query, kv = call(
        project_kernel,
        [shape((tokens, 2 * block), HALF), shape((tokens, 4 * block), HALF)],
        [h_one, h_one_far] + qkv + [row_m, row_s],
    )
    query, kv, cqo_got, far_rows = tie(query, kv, cqo_got, far_rows)
    cqo_got_x = to_x(cqo_got)
    kv_far = to_core(kv)
    mid = part // 2
    up_got = [to_y(up_own[:mid]), to_y(up_own[mid:])]
    attended, lse = call(
        attend_kernel,
        [shape((tokens, 2 * block), HALF), shape((2 * block // HD, tokens), FLOAT)],
        [query, kv, kv_far],
    )
    attended, o_got, cqo_x, ckv_got, text_got = tie(attended, o_got, cqo_x, ckv_got, text_got)
    (text_two,) = call(
        text_kernel, [shape((text_rows, 2 * block), HALF)], [text_own, text_got, ckv_own, ckv_got, row_m]
    )
    attended, text_two = tie(attended, text_two)
    outs = [o_own, o_got, o_core, to_core(o_got)]
    attn_near, attn_far = call(out_kernel, [pair_wide, pair_half], [attended] + outs)
    attn_far = to_x(attn_far)
    gradient = tokens_sent(cotangent, y)
    down_got = [to_y(down_own[:mid]), to_y(down_own[mid:])]

    text_near = cat((text_two, to_core(text_two)), 1)
    text_far = to_x(text_near)
    attn_far, text_far, cqo_got_x, up_got[0] = tie(attn_far, text_far, cqo_got_x, up_got[0])
    cqo_all = (
        cqo_own,
        cqo_got,
        to_core(cqo_own),
        to_core(cqo_got),
        cqo_x,
        cqo_got_x,
        to_core(cqo_x),
        to_core(cqo_got_x),
    )

    attn_out, cross_in, cross_query, cross_att, cross_lse, x_two, h_two = call(
        cross_kernel,
        [
            pair_wide,
            pair_half,
            shape((4, own, block), HALF),
            shape((4, own, block), HALF),
            shape((D // HD, own), FLOAT),
            pair_wide,
            pair_half,
        ],
        [latents, mods, attn_near, attn_far, row_m, row_s, far_rows, text_near, text_far, *cqo_all],
    )

    h_two, up_got[1] = tie(h_two, up_got[1])
    up_got = cat(up_got, 0)
    h_two_far = to_x(h_two)
    h_two_far, *gradient = tie(h_two_far, *gradient)
    gradient = tokens_got(*gradient, same)
    grad_mlp = half(cat((mods[0, 5:6], mods[1, 5:6]), 1) * wide(gradient))
    grad_mlp_far = to_x(grad_mlp)
    up = [up_own, up_got, up_core, to_core(up_got)]
    pre, hidden = call(
        up_kernel,
        [shape((2, tokens, ff), FLOAT), shape((2, tokens, ff), HALF)],
        [h_two, h_two_far] + up + [row_m, row_s],
    )
    hidden, grad_mlp_far, down_got[0] = tie(hidden, grad_mlp_far, down_got[0])

    ff_shape = shape((part, ff), HALF)
    down_keep, down_keep1, down_send, down_send1 = call(
        ff_weight_kernel, [ff_shape] * 4, [grad_mlp, grad_mlp_far, hidden]
    )
    down_keep, down_keep1, down_send, down_send1, down_got[1] = tie(
        down_keep, down_keep1, down_send, down_send1, down_got[1]
    )
    down_got = cat(down_got, 0)
    down_far = to_y(half(wide(down_keep1) + wide(to_core(down_send1))))
    down_keep = half(wide(down_keep) + wide(to_core(down_send)))
    down = [down_own, down_got, down_core, to_core(down_got)]
    grad_pre, two_near, two_far, pre_sums = call(
        mlp_back_kernel,
        [shape((2, tokens, ff), HALF), pair_wide, pair_half, shape((2, ff), FLOAT)],
        [grad_mlp, grad_mlp_far, pre] + up + down,
    )
    two_far = to_x(two_far)
    up_keep, up_keep1, up_send, up_send1 = call(
        ff_weight_kernel, [ff_shape] * 4, [h_two, h_two_far, grad_pre]
    )
    mlp_near, mlp_far = call(down_kernel, [pair_wide, pair_half], [hidden] + down)
    mlp_far, two_far, up_keep, up_keep1, up_send, up_send1 = tie(
        mlp_far, two_far, up_keep, up_keep1, up_send, up_send1
    )
    up_far = to_y(half(wide(up_keep1) + wide(to_core(up_send1))))
    up_keep = half(wide(up_keep) + wide(to_core(up_send)))

    text_shape = shape((text_rows, 4 * block), HALF)
    grad_cross, grad_cq, text_grad_near, text_grad_far, grad_x_one, grad_attn, cross_sums = call(
        cross_back_kernel,
        [
            pair_half,
            shape((4, own, block), HALF),
            text_shape,
            text_shape,
            pair_wide,
            pair_half,
            shape((2, 5, part), FLOAT),
        ],
        [gradient, mods, x_two, two_near, two_far, attn_out, cross_query, cross_lse, text_near, text_far, *cqo_all],
        [pltpu.VMEM((own, block), HALF)],
    )
    grad_attn, down_far = tie(grad_attn, down_far)
    grad_attn_far = to_x(grad_attn)
    down_sum = lax.psum(half(wide(down_keep) + wide(down_far)), "dp")
    cqo_shape = shape((block, 2 * D), HALF)
    cqo_keep, cqo_keep_x, cqo_send, cqo_send_x = call(
        cross_weight_kernel, [cqo_shape] * 4, [cross_in, grad_cross, grad_cq, cross_att]
    )
    text_grad_core = to_core(cat((text_grad_near[:, 2 * block :], text_grad_far[:, 2 * block :]), 1))
    cqo_keep = half(wide(cqo_keep) + wide(to_core(cqo_send)))
    cqo_far = half(wide(cqo_keep_x) + wide(to_core(cqo_send_x)))
    text_chip = half(
        wide(cat((text_grad_near[:, : 2 * block], text_grad_far[:, : 2 * block]), 1))
        + wide(text_grad_core)
    )
    grad_attn_far, cqo_far, text_chip = tie(grad_attn_far, cqo_far, text_chip)

    cqo_far = to_x(cqo_far)
    text_from = to_x(text_chip[:, 2 * block :])
    o_shape = shape((block, D), HALF)
    grad_att, o_keep, o_send = call(
        out_back_kernel,
        [shape((tokens, 2 * block), HALF), o_shape, o_shape],
        [grad_attn, grad_attn_far, attended] + outs,
    )
    mlp_far = to_x(mlp_far)
    grad_query, kv_keep, kv_send = call(
        attend_back_kernel,
        [
            shape((tokens, 2 * block), HALF),
            shape((tokens, 4 * block), FLOAT),
            shape((tokens, 4 * block), HALF),
        ],
        [query, kv, kv_far, lse, grad_att],
    )
    grad_query, kv_keep, kv_send, mlp_far, cqo_far, text_from, up_far, down_sum = tie(
        grad_query, kv_keep, kv_send, mlp_far, cqo_far, text_from, up_far, down_sum
    )
    up_sum = lax.psum(half(wide(up_keep) + wide(up_far)), "dp")
    kv_got = to_core(kv_send)
    rest_shape = shape((block, 5 * part), HALF)
    rest_keep, rest_far, grad_text, text_part, cv_sum = call(
        rest_kernel,
        [
            rest_shape,
            rest_shape,
            shape((text_rows, 2 * block), HALF),
            shape((text_rows, D), HALF),
            shape((1, block), FLOAT),
        ],
        [
            cqo_keep,
            cqo_far,
            text_chip[:, : 2 * block],
            text_from,
            text_own,
            text_got,
            ckv_own,
            ckv_got,
            o_keep,
            to_core(o_send),
        ],
    )
    rest_far = to_y(rest_far)
    layer_pair, layer_sums = call(
        layer_out_kernel,
        [pair_half, shape((2, 2, part), FLOAT)],
        [mlp_near, mlp_far, x_two, mods, gradient, grad_mlp],
    )
    layer_pair = halves_sent(layer_pair, same)
    text_near = to_core(text_part)
    grad_shape = shape((tokens, 3 * block), HALF)
    near, far, grad_m, grad_s, qkv_sums = call(
        project_back_kernel,
        [pair_wide, pair_half, grad_shape, grad_shape, shape((2, 3 * block), FLOAT)],
        [grad_query, kv_keep, kv_got] + qkv,
    )
    far, text_near = tie(far, text_near)
    far = to_x(far)
    text_sum = wide(text_part) + wide(text_near)
    text_got = to_x(half(text_sum))
    qkv_shape = shape((block, 3 * part), HALF)
    qkv_keep, qkv_keep1, qkv_send, qkv_send1 = call(
        project_weight_kernel, [qkv_shape] * 4, [h_one, h_one_far, grad_m, grad_s]
    )
    qkv_send, qkv_send1, qkv_keep, qkv_keep1, text_got, far, rest_far = tie(
        qkv_send, qkv_send1, qkv_keep, qkv_keep1, text_got, far, rest_far
    )
    rest_sum = DpSum(half(wide(rest_keep) + wide(rest_far)))
    rest_sum.send()
    qkv_far = to_y(half(wide(qkv_keep1) + wide(to_core(qkv_send1))))
    qkv_keep = half(wide(qkv_keep) + wide(to_core(qkv_send)))
    text_sum = text_sum + wide(text_got)
    text_far = to_y(half(text_sum[:, part:]))
    token_pair, one_sums = call(
        norm_back_kernel,
        [pair_half, shape((2, 2, part), FLOAT)],
        [latents, mods, near, far, grad_x_one],
    )
    token_pair, one_sums, qkv_far = tie_sums([rest_sum], token_pair, one_sums, qkv_far)
    qkv_sum = DpSum(half(wide(qkv_keep) + wide(qkv_far)))
    qkv_sum.send()
    rest_sum.send()
    token_sent = halves_sent(token_pair, same)

    feature_sums = cat((one_sums, cross_sums, layer_sums), 1)
    flat = feature_sums.reshape(9 * D)
    gcq_sum = jnp.sum(wide(grad_cq), 1)
    cv_sum = cv_sum[0]
    core_got = to_core(
        cat((flat, gcq_sum[3], gcq_sum[1], qkv_sums[1, :block], qkv_sums[1, 2 * block :], pre_sums[1]), 0)
    )
    core_got, text_far = tie_sums([qkv_sum, rest_sum], core_got, text_far)
    qkv_sum.send()
    rest_sum.send()
    text_grad = in_order(text_sum[:, :part], wide(text_far))
    chip = core_got + cat(
        (flat, gcq_sum[2], gcq_sum[0], qkv_sums[0, :block], qkv_sums[0, 2 * block :], pre_sums[0]), 0
    )
    x_got = to_x(chip[: 9 * D + block])
    x_got, up_sum = tie_sums([qkv_sum, rest_sum], x_got, up_sum)
    qkv_sum.send()
    rest_sum.send()
    sums = (chip[: 9 * D] + x_got[: 9 * D]).reshape(2, 9, part)
    cq_row = chip[9 * D + block : 9 * D + 2 * block] + x_got[9 * D :]
    rest = chip[9 * D + 2 * block :]
    row_rows = [
        (v[: v.shape[0] // 2], v[v.shape[0] // 2 :])
        for v in (rest[:block], rest[block : 2 * block], cq_row, cv_sum, rest[2 * block :])
    ]
    row_low = cat([v[0] for v in row_rows], 0)
    row_high = cat([v[1] for v in row_rows], 0)
    row_mine = jnp.where(first_col, row_low, row_high)
    row_sent = jnp.where(first_col, row_high, row_low)
    col_got = to_y(cat((sums[1].reshape(9 * part), row_sent), 0))
    col_got, *both = tie_sums([qkv_sum, rest_sum], col_got, *token_sent, *layer_pair)
    qkv_sum.send()
    rest_sum.send()
    token_input_gradient = wide(halves_got(*both[:2], y))
    layer_out = halves_got(*both[2:], y)
    sums_got = col_got[: 9 * part].reshape(9, part)
    sums_own = sums[0]

    def six(v):
        return jnp.stack((v[0], v[1], v[5], v[2], v[3], v[7]))

    time_own, time_got = six(sums_own), six(sums_got)
    time_grad = jnp.where(first_col, jnp.stack((time_own, time_got)), jnp.stack((time_got, time_own)))
    totals = small_sum_over_dp(
        cat(((sums_own + sums_got).reshape(9 * part), row_mine + col_got[9 * part :]), 0)
    )
    table_grad = six(totals[: 9 * part].reshape(9, part))
    o_bias_grad, co_bias_grad, down_bias_grad = (
        totals[i * part : (i + 1) * part] for i in (6, 4, 8)
    )
    rows = totals[9 * part :]
    q_bias_grad, v_bias_grad, cq_bias_grad, cv_bias_grad = (
        rows[i * quarter : (i + 1) * quarter] for i in range(4)
    )
    up_bias_grad = rows[4 * quarter :]

    qkv_grad, rest_sum = qkv_sum.finish(), rest_sum.finish()
    q_grad, k_grad, v_grad = (wide(qkv_grad[:, i * part : (i + 1) * part]).T for i in range(3))
    cq_grad, co_grad, ck_grad, cv_grad, o_grad = (
        wide(rest_sum[:, i * part : (i + 1) * part]) for i in range(5)
    )
    return (
        layer_out,
        token_input_gradient,
        text_grad,
        time_grad,
        table_grad,
        q_grad,
        k_grad,
        v_grad,
        q_bias_grad,
        v_bias_grad,
        o_grad,
        o_bias_grad,
        cq_grad.T,
        cq_bias_grad,
        ck_grad.T,
        cv_grad.T,
        cv_bias_grad,
        co_grad,
        co_bias_grad,
        wide(up_sum),
        up_bias_grad,
        wide(down_sum).T,
        down_bias_grad,
    )


def solution(mesh):
    in_specs = (
        P(("dp", "row"), "col"),
        P("dp", "col"),
        P("dp", None, "col"),
        P(None, "col"),
        P("col", "row"),
        P("col", "row"),
        P("col", "row"),
        P(("row", "col")),
        P(("row", "col")),
        P("row", "col"),
        P("col"),
        P("col", "row"),
        P(("row", "col")),
        P("col", "row"),
        P("col", "row"),
        P(("row", "col")),
        P("row", "col"),
        P("col"),
        P("col", "row"),
        P(("row", "col")),
        P("row", "col"),
        P("col"),
        P(("dp", "row"), "col"),
    )
    out_specs = (
        P(("dp", "row"), "col"),
        P(("dp", "row"), "col"),
        P("dp", "col"),
        P("dp", None, "col"),
        P(None, "col"),
        P("col", "row"),
        P("col", "row"),
        P("col", "row"),
        P(("row", "col")),
        P(("row", "col")),
        P("row", "col"),
        P("col"),
        P("col", "row"),
        P(("row", "col")),
        P("col", "row"),
        P("col", "row"),
        P(("row", "col")),
        P("row", "col"),
        P("col"),
        P("col", "row"),
        P(("row", "col")),
        P("row", "col"),
        P("col"),
    )
    return jax.shard_map(
        on_device, mesh=mesh, in_specs=in_specs, out_specs=out_specs, check_vma=False
    )
```
